256 devices in a mesh: tm: 64 (over y, x_hi, z), tp: 4 (over x_lo, core).
Axes of the slice: x: 4 (x_hi: 2, x_lo: 2; x = x_hi * 2 + x_lo), y: 4, z: 8, core: 2. Of those that a mesh axis runs over, the one named last changes fastest.
Arguments:
- queries: bfloat16 [32768, 2560], P('tm', 'tp'), may hold values from -24 to 24
- key_rows: bfloat16 [32768, 2560], P('tm', 'tp'), may hold values from -24 to 24
- value_rows: bfloat16 [32768, 2560], P('tm', 'tp'), may hold values from -6 to 6
- query_gain: float32 [2560], P('tp'), may hold values from 0.1 to 1.9
- key_gain: float32 [2560], P('tp'), may hold values from 0.1 to 1.9
- out_weight: bfloat16 [2560, 5120], P('tp'), may hold values from -0.5 to 0.5
- residual: bfloat16 [32768, 5120], P('tm', 'tp'), may hold values from -3 to 3
- gate_table: bfloat16 [50, 5120], P(None, 'tp'), may hold values from -8 to 8
- timesteps: int32 [64], P('tm'), may hold values from 0 to 49
- windows: int32 [64], P('tm'), may hold values from 1 to 4, as said below
- queue_positions: int32 [64], P('tm'), may hold values from 0 to 63, as said below
- fresh_span: bfloat16 [512, 5120], P(None, 'tp'), may hold values from -6 to 6
Outputs:
- advanced: bfloat16 [32768, 5120], P('tm', 'tp')
The draws below stay inside these ranges and needn't reach their ends.
Inputs may be any that keep to these rules, and one draw needn't show every extreme that they name: `windows`: some span whose queue position is at most 59 has the value 4. A rotation: queue_positions[c] = (c - s) mod 64 for one slot s.
All inputs are finite; a program needn't handle non-finite values.
Results may differ from the reference program's by a relative error of at most 0.015.
Values may be sent and summed in bfloat16 or wider, within the bound.
A program may use at most 128 MiB of HBM per device.

```python
import jax
import jax.numpy as jnp
from jax import lax

D = 5120
HEADS = 20
HD = 128
ROWS = 512
WMAX = 4
STEPS = 50
SPANS = 64
TOKENS = 32768
WIDTH = 2560
N_TP = 4


def column_scale(key):
    column = jnp.arange(WIDTH, dtype=jnp.float32)
    return jnp.sqrt(1.0 + 2.0 * column / WIDTH) * jnp.exp(jax.random.uniform(key, (WIDTH,), jnp.float32, -1.15, 1.15))


def queue_layout(key):
    first, second, third = jax.random.split(key, 3)
    start = jax.random.randint(first, (), 0, SPANS)
    offset = jax.random.randint(second, (), 0, SPANS - WMAX)
    reaches = jax.random.randint(third, (SPANS,), 1, WMAX + 1)
    chosen = (start + offset) % SPANS
    reaches = jnp.where(jnp.arange(SPANS) == chosen, WMAX, reaches)
    return (start, reaches)


def draw_queries(key, part):
    key = jax.random.fold_in(key, 7)
    first, second, third = jax.random.split(key, 3)
    noise = jnp.clip(jax.random.normal(first, (TOKENS, WIDTH), jnp.float32), -4.0, 4.0)
    row_scale = jnp.exp(jax.random.uniform(second, (TOKENS,), jnp.float32, 0.0, 2.3))
    field = noise * row_scale[:, None] * column_scale(third)[None, :] / 4.0
    return jnp.clip(field, -24.0, 24.0).astype(jnp.bfloat16)


def draw_key_rows(key, part):
    key = jax.random.fold_in(key, 9)
    first, second, third = jax.random.split(key, 3)
    noise = jnp.clip(jax.random.normal(first, (TOKENS, WIDTH), jnp.float32), -4.0, 4.0)
    row_scale = jnp.exp(jax.random.uniform(second, (TOKENS,), jnp.float32, 0.0, 2.3))
    field = noise * row_scale[:, None] * column_scale(third)[None, :] / 4.0
    return jnp.clip(field, -24.0, 24.0).astype(jnp.bfloat16)


def draw_windows(key, part):
    start, reaches = queue_layout(key)
    return reaches.astype(jnp.int32)


def draw_queue_positions(key, part):
    start, reaches = queue_layout(key)
    return ((jnp.arange(SPANS, dtype=jnp.int32) - start) % SPANS).astype(jnp.int32)


def plant(entries, rng, smallest, largest):
    dims = entries.shape
    spot = [jax.random.randint(jax.random.fold_in(rng, axis), (), 0, dims[axis]) for axis in range(len(dims))]
    entries = entries.at[tuple(spot)].set(smallest)
    longest = dims.index(max(dims))
    spot[longest] = (spot[longest] + 1) % dims[longest]
    return entries.at[tuple(spot)].set(largest)


def block_levels(stream_key, extent, shards, low, high):
    level = 1.0
    for dim, blocks in shards:
        heights = jax.random.uniform(jax.random.fold_in(jax.random.fold_in(stream_key, 6), dim), (blocks,), jnp.float32, low / len(shards), high / len(shards))
        level = level * jnp.repeat(jnp.exp(heights), extent[dim] // blocks).reshape((-1,) + (1,) * (len(extent) - 1 - dim))
    return level


def bell_draw(stream_key, extent, scale, reach, cuts=(), kind=jnp.bfloat16):
    values = scale * jax.random.normal(stream_key, extent, jnp.float32)
    if cuts:
        values = values * block_levels(stream_key, extent, cuts, -0.22, 0.18)
    return jnp.clip(values, -reach, reach).astype(kind)


def setup_inputs(seed: int = 0) -> dict:
    streams_of = jax.random.split(jax.random.key(seed), 13)
    return {
        "queries": draw_queries(jax.random.fold_in(streams_of[12], 71), 0),
        "key_rows": draw_key_rows(jax.random.fold_in(streams_of[12], 71), 0),
        "value_rows": bell_draw(streams_of[2], (TOKENS, WIDTH), 1.0, 6.0, ((0, 64), (1, 4))),
        "query_gain": jnp.clip(1.0 + 0.18 * jax.random.normal(streams_of[3], (WIDTH,), jnp.float32), 0.1, 1.9),
        "key_gain": jnp.clip(1.0 + 0.18 * jax.random.normal(streams_of[4], (WIDTH,), jnp.float32), 0.1, 1.9),
        "out_weight": bell_draw(streams_of[5], (WIDTH, D), HD ** -0.5, 0.5, ((0, 4),)),
        "residual": bell_draw(streams_of[6], (TOKENS, D), 0.5, 3.0, ((0, 64), (1, 4))),
        "gate_table": bell_draw(streams_of[7], (STEPS, D), 1.5, 8.0, ((1, 4),)),
        "timesteps": plant(jax.random.randint(streams_of[8], (SPANS,), 0, STEPS), jax.random.fold_in(streams_of[8], 1), 0, STEPS - 1).astype(jnp.int32),
        "windows": draw_windows(jax.random.fold_in(streams_of[12], 71), 0),
        "queue_positions": draw_queue_positions(jax.random.fold_in(streams_of[12], 71), 0),
        "fresh_span": bell_draw(streams_of[11], (ROWS, D), 1.0, 6.0, ((1, 4),)),
    }


epsilon = 1e-06

def normalize(field, gain):
    wide = field.astype(jnp.float32)
    energy = lax.optimization_barrier(jnp.mean(wide * wide, axis=1, keepdims=True))
    return (wide * lax.rsqrt(energy + epsilon) * gain[None, :]).astype(jnp.bfloat16)

def reference(queries, key_rows, value_rows, query_gain, key_gain, out_weight, residual, gate_table, timesteps, windows, queue_positions, fresh_span):
    width = HEADS * HD
    group = width // N_TP
    query_norm = normalize(queries, query_gain).reshape(SPANS, ROWS, HEADS, HD)
    key_norm = normalize(key_rows, key_gain).reshape(SPANS, ROWS, HEADS, HD)
    value_blocks = value_rows.reshape(SPANS, ROWS, HEADS, HD)
    resid_blocks = residual.reshape(SPANS, ROWS, D)

    def one_span(span):
        position = queue_positions[span]
        key_list = []
        value_list = []
        mask_list = []
        for distance in range(WMAX + 1):
            source = ((span + distance) % SPANS).astype(jnp.int32)
            key_list.append(lax.dynamic_index_in_dim(key_norm, source, 0, keepdims=False))
            value_list.append(lax.dynamic_index_in_dim(value_blocks, source, 0, keepdims=False))
            if distance == 0:
                allowed = jnp.array(True)
            else:
                allowed = jnp.logical_and(distance <= windows[span], position + distance <= SPANS - 1)
            mask_list.append(jnp.broadcast_to(allowed, (ROWS,)))
        keys_all = jnp.concatenate(key_list, 0).astype(jnp.float32)
        values_all = jnp.concatenate(value_list, 0).astype(jnp.float32)
        live = jnp.concatenate(mask_list, 0)
        query_here = lax.dynamic_index_in_dim(query_norm, span, 0, keepdims=False).astype(jnp.float32)
        scores = jnp.einsum('qhd,khd->hqk', query_here, keys_all) * HD ** (-0.5)
        scores = jnp.where(live[None, None, :], scores, -jnp.inf)
        peak = lax.optimization_barrier(jnp.max(scores, axis=2, keepdims=True))
        expo = jnp.exp(scores - peak)
        total = lax.optimization_barrier(jnp.sum(expo, axis=2, keepdims=True))
        weight = expo.astype(jnp.bfloat16)
        mixed = jnp.einsum('hqk,khd->hqd', weight.astype(jnp.float32), values_all) / total
        attended = jnp.transpose(mixed, (1, 0, 2)).reshape(ROWS, width).astype(jnp.bfloat16)
        projected = jnp.zeros((ROWS, D), jnp.float32)
        for member in range(N_TP):
            partial_value = jnp.dot(attended[:, member * group:(member + 1) * group], out_weight[member * group:(member + 1) * group], preferred_element_type=jnp.float32)
            projected = projected + partial_value.astype(jnp.bfloat16).astype(jnp.float32)
        gate = lax.dynamic_index_in_dim(gate_table, timesteps[span].astype(jnp.int32), 0, keepdims=False).astype(jnp.float32)
        resid_here = lax.dynamic_index_in_dim(resid_blocks, span, 0, keepdims=False).astype(jnp.float32)
        return (resid_here + gate[None, :] * projected).astype(jnp.bfloat16)
    updated = lax.map(one_span, jnp.arange(SPANS, dtype=jnp.int32))
    moved = jnp.roll(updated, 1, axis=0)
    newest = queue_positions == 0
    result = jnp.where(newest[:, None, None], fresh_span[None, :, :], moved)
    return result.reshape(SPANS * ROWS, D)
```

```python
import jax
import jax.numpy as jnp
from jax import lax
from jax.experimental import pallas as pl
from jax.experimental.pallas import tpu as pltpu
from jax.sharding import PartitionSpec as P

HD = 128
WMAX = 4
EPS = 1e-06
FEW = -1e30
MANY = 1e30
LOG2E = 1.4426950408889634
MESH = pl.DeviceIdType.MESH
F32 = jnp.float32
BF16 = jnp.bfloat16


def kernel(
    spans,
    q_hbm,
    k_hbm,
    v_hbm,
    gain_ref,
    w_hbm,
    res_hbm,
    gate_ref,
    step_ref,
    reach_ref,
    pos_ref,
    out_ref,
    q_own,
    k_own,
    v_own,
    vt_own,
    qn,
    kn,
    qa,
    qb,
    k1,
    vt1,
    k2,
    vt2,
    est,
    st_own,
    st_in,
    os_out,
    os_stat,
    os_in,
    os_in_stat,
    far_out,
    far_stat,
    far_in,
    far_in_stat,
    acc,
    top,
    ag,
    wbuf,
    res,
    total,
    load_sem,
    wload_sem,
    est_s,
    est_r,
    st_s,
    st_r,
    q_s,
    q_r,
    qf_s,
    qf_r,
    k_s,
    k_r,
    v_s,
    v_r,
    kf_s,
    kf_r,
    vf_s,
    vf_r,
    os_s,
    os_r,
    oss_s,
    oss_r,
    far_s,
    far_r,
    fars_s,
    fars_r,
    res_s,
    res_r,
    wsib_s,
    wsib_r,
    wx_s,
    wx_r,
    wy_s,
    wy_r,
    ag_s,
    ag_r,
):
    heads, rows = q_own.shape[0], q_own.shape[1]
    local = heads * HD
    width = 4 * local
    out_cols = out_ref.shape[1]
    half_cols = out_cols // 2
    tm = lax.axis_index("tm")
    tp = lax.axis_index("tp")
    lo, core = tp // 2, tp % 2
    x_hi, y, z = (tm // 8) % 2, tm // 16, tm % 8

    def shifted(by):
        return (lax.rem(tm + by + spans, spans), tp)

    peers = [(tm, lax.rem(tp + by, 4)) for by in (1, 2, 3)]
    across = [(tm + 8 - 16 * x_hi, (1 - lo) * 2 + c) for c in (0, 1)]
    turn = jnp.where(z >= 4, -16, 16)
    y_next, y_prev = shifted(turn), shifted(-turn)
    turn_y = turn // 16

    def load(src, dst, slot, h):
        return pltpu.make_async_copy(
            src.at[:, pl.ds(pl.multiple_of(h * HD, HD), HD)], dst.at[h], load_sem.at[slot, h]
        )

    loads = [(q_hbm, q_own, 0), (k_hbm, k_own, 1), (v_hbm, v_own, 2)]
    for src, dst, slot in loads:
        for h in range(heads):
            load(src, dst, slot, h).start()

    barrier = pltpu.get_barrier_semaphore()
    greet = [shifted(1), shifted(-1), shifted(2), shifted(-2)] + peers + across + [y_prev]
    for other in greet:
        pl.semaphore_signal(barrier, inc=1, device_id=other, device_id_type=MESH)

    w_own_copy = pltpu.make_async_copy(
        w_hbm.at[:, :, pl.ds(pl.multiple_of(tp * out_cols, HD), out_cols)],
        wbuf.at[:, pl.ds(pl.multiple_of(tp * HD, HD), HD), :],
        wload_sem,
    )
    w_own_copy.start()

    ones = jnp.ones((16, rows), BF16)
    for h in range(heads):
        vt_own[h, HD : HD + 16, :] = ones
        vt1[h, HD : HD + 16, :] = ones
        vt2[h, HD : HD + 16, :] = ones

    def energy_of(ref, slot, src):
        squares = jnp.zeros((rows, HD), F32)
        for h in range(heads):
            load(src, ref, slot, h).wait()
            wide = ref[h].astype(F32)
            squares = squares + wide * wide
        return jnp.sum(jnp.transpose(squares), axis=0, keepdims=True)

    energy_q = energy_of(q_own, 0, q_hbm)
    energy_k = energy_of(k_own, 1, k_hbm)
    line = lax.broadcasted_iota(jnp.int32, (8, rows), 0)
    message = jnp.where(line == 0, energy_q, 0.0)
    message = jnp.where(line == 1, energy_k, message)
    message = jnp.where(line == 2, reach_ref[0].astype(F32) * 0.25, message)
    message = jnp.where(line == 3, step_ref[0].astype(F32) * 0.25, message)
    est[tp] = message

    for h in range(heads):
        load(v_hbm, v_own, 2, h).wait()
        vt_own[h, :HD, :] = jnp.transpose(v_own[h])

    pl.semaphore_wait(barrier, len(greet))

    def remote(src, dst, send, recv, to):
        return pltpu.make_async_remote_copy(
            src_ref=src, dst_ref=dst, send_sem=send, recv_sem=recv, device_id=to, device_id_type=MESH
        )

    up, down = shifted(1), shifted(-1)
    est_copies = [
        remote(est.at[tp], est.at[tp], est_s.at[i], est_r.at[tp], to) for i, to in enumerate(peers)
    ]

    def est_in(i):
        who = lax.rem(tp + i + 1, 4)
        return remote(est.at[who], est.at[who], est_s.at[i], est_r.at[who], peers[i])

    def q_copy(h):
        return remote(q_own.at[h], qa.at[h], q_s.at[h], q_r.at[h], up)

    def q_forward(h):
        return remote(qa.at[h], qb.at[h], qf_s.at[h], qf_r.at[h], up)

    def k_copy(h):
        return remote(k_own.at[h], k1.at[h], k_s.at[h], k_r.at[h], down)

    def v_copy(h):
        return remote(
            vt_own.at[h, pl.ds(0, HD), :], vt1.at[h, pl.ds(0, HD), :], v_s.at[h], v_r.at[h], down
        )

    def k_forward(h):
        return remote(k1.at[h], k2.at[h], kf_s.at[h], kf_r.at[h], down)

    def v_forward(h):
        return remote(
            vt1.at[h, pl.ds(0, HD), :], vt2.at[h, pl.ds(0, HD), :], vf_s.at[h], vf_r.at[h], down
        )

    def os_copy(h):
        return remote(os_out.at[h], os_in.at[h], os_s.at[h], os_r.at[h], up)

    def os_stat_copy(h):
        return remote(os_stat.at[h], os_in_stat.at[h], oss_s.at[h], oss_r.at[h], up)

    def far_copy(h):
        return remote(far_out.at[h], far_in.at[h], far_s.at[h], far_r.at[h], down)

    def far_stat_copy(h):
        return remote(far_stat.at[h], far_in_stat.at[h], fars_s.at[h], fars_r.at[h], down)

    parts = res_s.shape[0]
    part_rows = rows // parts

    def res_copy(i):
        cut = pl.ds(i * part_rows, part_rows)
        return remote(res_hbm.at[cut], res.at[cut], res_s.at[i], res_r.at[i], up)

    def st_copy(i, by):
        return remote(st_own, st_in.at[i], st_s.at[i], st_r.at[i], shifted(by))

    sibling = (tm, lo * 2 + 1 - core)

    def w_slot(h, who, half):
        return wbuf.at[
            h,
            pl.ds(pl.multiple_of(who * HD, HD), HD),
            pl.ds(pl.multiple_of(half * half_cols, HD), half_cols),
        ]

    def w_sibling():
        return remote(
            w_hbm.at[:, :, pl.ds(pl.multiple_of(sibling[1] * out_cols, HD), out_cols)],
            wbuf.at[:, pl.ds(pl.multiple_of(tp * HD, HD), HD), :],
            wsib_s,
            wsib_r,
            sibling,
        )

    def w_across(c, h):
        column = across[c][1] * out_cols + lax.rem(y, 2) * half_cols
        return remote(
            w_hbm.at[h, :, pl.ds(pl.multiple_of(column, HD), half_cols)],
            w_slot(h, tp, lax.rem(y, 2)),
            wx_s.at[c, h],
            wx_r.at[h],
            across[c],
        )

    def w_piece(piece, h):
        return w_slot(h, (1 - lo) * 2 + piece // 2, lax.rem(piece, 2))

    def w_across_in(h):
        slot = w_piece(y, h)
        return remote(slot, slot, wx_s.at[0, h], wx_r.at[h], across[0])

    def w_along(k, h):
        slot = w_piece(lax.rem(y - turn_y * k + 4, 4), h)
        return remote(slot, slot, wy_s.at[k, h], wy_r.at[k, h], y_next)

    def w_along_in(k, h):
        slot = w_piece(lax.rem(y - turn_y * (k + 1) + 8, 4), h)
        return remote(slot, slot, wy_s.at[k, h], wy_r.at[k, h], y_next)

    def ag_slot(h, who):
        return ag.at[h, :, pl.ds(pl.multiple_of(who * HD, HD), HD)]

    def ag_copy(i, h):
        return remote(ag_slot(h, tp), ag_slot(h, tp), ag_s.at[i, h], ag_r.at[tp, h], peers[i])

    def ag_in(i, h):
        who = lax.rem(tp + i + 1, 4)
        return remote(ag_slot(h, who), ag_slot(h, who), ag_s.at[i, h], ag_r.at[who, h], peers[i])

    def each(body):
        @pl.loop(0, heads)
        def _(h):
            body(h)

    for copy in est_copies:
        copy.start()
    for h in range(2):
        q_copy(h).start()
        k_copy(h).start()
        v_copy(h).start()

    for i in range(3):
        est_in(i).wait_recv()
    st_own[...] = est[0] + est[1] + est[2] + est[3]
    st_moves = [(0, 1), (1, 2), (2, -1), (3, -2)]
    for i, by in st_moves:
        st_copy(i, by).start()

    @pl.loop(2, heads)
    def _(h):
        q_copy(h).start()
        k_copy(h).start()
        v_copy(h).start()

    @pl.when(core == y // 2)
    def _():
        @pl.loop(0, heads)
        def _(h):
            w_across(0, h).start()
            w_across(1, h).start()

    w_sibling().start()

    def column(state, row):
        scale = lax.rsqrt(state[row : row + 1, :] / width + EPS)
        return jnp.transpose(jnp.broadcast_to(scale, (HD, rows)))

    def unit_q(raw, scale, h):
        return (raw.astype(F32) * scale * gain_ref[pl.ds(h, 1), :]).astype(BF16)

    def unit_k(raw, scale):
        return (raw.astype(F32) * scale).astype(BF16)

    def scores_of(keys, queries):
        return lax.dot_general(
            keys, queries, (((1,), (1,)), ((), ())), preferred_element_type=F32
        )

    def alone(keys, queries, values):
        scores = scores_of(keys, queries)
        peak = jnp.max(scores, axis=0, keepdims=True)
        weight = jnp.exp2(scores - peak).astype(BF16)
        return jnp.dot(values, weight, preferred_element_type=F32), peak

    line_8 = lax.broadcasted_iota(jnp.int32, (8, rows), 0)

    def pair(first, second):
        return jnp.where(line_8 == 0, first, second)

    q_scale = column(st_own, 0)
    k_scale = column(st_own, 1)

    def self_part(h):
        q_copy(h).wait_recv()
        q_forward(h).start()
        kn[h] = unit_k(k_own[h], k_scale)
        mixed, peak = alone(kn[h], unit_q(q_own[h], q_scale, h), vt_own[h])
        os_out[h] = mixed[:HD].astype(BF16)
        os_stat[h] = pair(peak, mixed[HD : HD + 1])
        os_copy(h).start()
        os_stat_copy(h).start()

    each(self_part)
    for i in range(parts):
        res_copy(i).start()

    st_copy(0, 1).wait_recv()
    state_a = st_in.at[0]
    reach = state_a[2:3, :]
    step = state_a[3:4, :1]
    place = lax.rem(pos_ref[0] + spans - 1, spans)

    def live(distance):
        inside = (place + distance <= spans - 1).astype(F32)
        return jnp.logical_and(reach >= distance, inside > 0.5)

    qa_scale = column(state_a, 0)

    def near_part(h):
        qn[h] = unit_q(qa[h], qa_scale, h)
        scores = scores_of(kn[h], qn[h])
        allowed = live(1)
        peak = jnp.max(scores, axis=0, keepdims=True)
        weight = jnp.exp2(scores - jnp.where(allowed, peak, MANY)).astype(BF16)
        acc[h] = jnp.dot(vt_own[h], weight, preferred_element_type=F32)
        top[h] = jnp.broadcast_to(jnp.where(allowed, peak, FEW), (8, rows))

    each(near_part)

    def join(h, keys, values, allowed):
        scores = scores_of(keys, qn[h])
        before = top[h][:1]
        peak = jnp.where(allowed, jnp.max(scores, axis=0, keepdims=True), FEW)
        after = jnp.maximum(before, peak)
        weight = jnp.exp2(scores - jnp.where(allowed, after, MANY)).astype(BF16)
        acc[h] = acc[h] * jnp.exp2(before - after) + jnp.dot(
            values, weight, preferred_element_type=F32
        )
        top[h] = jnp.broadcast_to(after, (8, rows))

    st_copy(2, -1).wait_recv()
    k1_scale = column(st_in.at[2], 1)

    def second_part(h):
        k_copy(h).wait_recv()
        k_forward(h).start()
        v_copy(h).wait_recv()
        v_forward(h).start()
        join(h, unit_k(k1[h], k1_scale), vt1[h], live(2))
        w_across_in(h).wait_recv()
        w_along(0, h).start()

    each(second_part)

    st_copy(1, 2).wait_recv()
    st_copy(3, -2).wait_recv()
    qb_scale = column(st_in.at[1], 0)
    k2_scale = column(st_in.at[3], 1)

    def third_part(h):
        q_forward(h).wait_recv()
        k_forward(h).wait_recv()
        v_forward(h).wait_recv()
        keys = unit_k(k2[h], k2_scale)
        mixed, peak = alone(keys, unit_q(qb[h], qb_scale, h), vt2[h])
        far_out[h] = mixed[:HD].astype(BF16)
        far_stat[h] = pair(peak, mixed[HD : HD + 1])
        far_copy(h).start()
        far_stat_copy(h).start()
        join(h, keys, vt2[h], live(3))
        w_along_in(0, h).wait_recv()
        w_along(1, h).start()

    each(third_part)

    def project(h):
        for i in range(3):
            ag_in(i, h).wait_recv()
        w_along_in(2, h).wait_recv()

        @pl.loop(0, out_cols // 256)
        def _(j):
            cut = pl.ds(pl.multiple_of(j * 256, 256), 256)
            fresh = jnp.dot(ag[h], wbuf[h, :, cut], preferred_element_type=F32)
            total[:, cut] = total[:, cut] + fresh

    total[...] = jnp.zeros_like(total)

    def merge(h):
        w_along_in(1, h).wait_recv()
        w_along(2, h).start()
        os_copy(h).wait_recv()
        os_stat_copy(h).wait_recv()
        far_copy(h).wait_recv()
        far_stat_copy(h).wait_recv()
        state_s, state_f = os_in_stat[h], far_in_stat[h]
        peak_s, peak_m = state_s[:1], top[h][:1]
        peak_f = jnp.where(live(4), state_f[:1], FEW)
        peak = jnp.maximum(jnp.maximum(peak_s, peak_m), peak_f)
        by_s, by_m, by_f = jnp.exp2(peak_s - peak), jnp.exp2(peak_m - peak), jnp.exp2(peak_f - peak)
        mixed = acc[h]
        whole = state_s[1:2] * by_s + mixed[HD : HD + 1] * by_m + state_f[1:2] * by_f
        share = 1.0 / whole
        attended = (
            os_in[h].astype(F32) * (by_s * share)
            + mixed[:HD] * (by_m * share)
            + far_in[h].astype(F32) * (by_f * share)
        )
        ag[h, :, pl.ds(pl.multiple_of(tp * HD, HD), HD)] = jnp.transpose(attended).astype(BF16)
        for i in range(3):
            ag_copy(i, h).start()

    merge(0)
    w_own_copy.wait()
    w_sibling().wait_recv()

    @pl.loop(1, heads)
    def _(h):
        merge(h)
        project(h - 1)

    project(heads - 1)
    for i in range(parts):
        res_copy(i).wait_recv()
    table = gate_ref[...].astype(F32)
    pick = lax.broadcasted_iota(jnp.int32, table.shape, 0).astype(F32) == step
    gate = jnp.sum(jnp.where(pick, table, 0.0), axis=0, keepdims=True)
    out_ref[...] = (res[...].astype(F32) + gate * total[...]).astype(BF16)

    for copy in est_copies:
        copy.wait_send()
    for i, by in st_moves:
        st_copy(i, by).wait_send()
    for i in range(parts):
        res_copy(i).wait_send()
    w_sibling().wait_send()

    @pl.when(core == y // 2)
    def _():
        @pl.loop(0, heads)
        def _(h):
            w_across(0, h).wait_send()
            w_across(1, h).wait_send()

    def sent(h):
        for copy in (
            q_copy,
            q_forward,
            k_copy,
            v_copy,
            k_forward,
            v_forward,
            os_copy,
            os_stat_copy,
            far_copy,
            far_stat_copy,
        ):
            copy(h).wait_send()
        for i in range(3):
            w_along(i, h).wait_send()
            ag_copy(i, h).wait_send()

    each(sent)


def local(
    queries,
    key_rows,
    value_rows,
    query_gain,
    key_gain,
    out_weight,
    residual,
    gate_table,
    timesteps,
    windows,
    queue_positions,
    fresh_span,
):
    spans = lax.axis_size("tm")
    rows, width = queries.shape
    heads = width // HD
    out_cols = residual.shape[1]
    gain = (query_gain * key_gain * (HD ** (-0.5) * LOG2E)).reshape(heads, HD)
    weight = out_weight.reshape(heads, HD, out_weight.shape[1])
    chunk = pltpu.VMEM((heads, rows, HD), BF16)
    flat = pltpu.VMEM((heads, HD, rows), BF16)
    tall = pltpu.VMEM((heads, HD + 16, rows), BF16)
    stats = pltpu.VMEM((heads, 8, rows), F32)
    one = pltpu.SemaphoreType.DMA
    per_head = one((heads,))
    parts = 4
    hbm = pl.BlockSpec(memory_space=pl.ANY)
    vmem = pl.BlockSpec(memory_space=pltpu.VMEM)
    smem = pl.BlockSpec(memory_space=pltpu.SMEM)

    def run(*operands):
        def body(*refs):
            kernel(spans, *refs)

        return pl.pallas_call(
            body,
            out_shape=jax.ShapeDtypeStruct((rows, out_cols), BF16),
            in_specs=[hbm, hbm, hbm, vmem, hbm, hbm, vmem, smem, smem, smem],
            out_specs=vmem,
            scratch_shapes=[
                chunk,
                chunk,
                chunk,
                tall,
                chunk,
                chunk,
                chunk,
                chunk,
                chunk,
                tall,
                chunk,
                tall,
                pltpu.VMEM((4, 8, rows), F32),
                pltpu.VMEM((8, rows), F32),
                pltpu.VMEM((4, 8, rows), F32),
                flat,
                stats,
                flat,
                stats,
                flat,
                stats,
                flat,
                stats,
                pltpu.VMEM((heads, HD + 16, rows), F32),
                stats,
                pltpu.VMEM((heads, rows, 4 * HD), BF16),
                pltpu.VMEM((heads, 4 * HD, out_cols), BF16),
                pltpu.VMEM((rows, out_cols), BF16),
                pltpu.VMEM((rows, out_cols), F32),
                one((3, heads)),
                one,
                one((3,)),
                one((4,)),
                one((4,)),
                one((4,)),
                per_head,
                per_head,
                per_head,
                per_head,
                per_head,
                per_head,
                per_head,
                per_head,
                per_head,
                per_head,
                per_head,
                per_head,
                per_head,
                per_head,
                per_head,
                per_head,
                per_head,
                per_head,
                per_head,
                per_head,
                one((parts,)),
                one((parts,)),
                one,
                one,
                one((2, heads)),
                per_head,
                one((3, heads)),
                one((3, heads)),
                one((3, heads)),
                one((4, heads)),
            ],
            compiler_params=pltpu.CompilerParams(
                collective_id=0, has_side_effects=True, vmem_limit_bytes=56 * 2**20
            ),
            name="window_block",
        )(*operands)

    updated = run(
        queries,
        key_rows,
        value_rows,
        gain,
        weight,
        residual,
        gate_table,
        timesteps,
        windows,
        queue_positions,
    )
    return jnp.where(queue_positions[0] == 0, fresh_span, updated)


def solution(mesh):
    placed = (
        P("tm", "tp"),
        P("tm", "tp"),
        P("tm", "tp"),
        P("tp"),
        P("tp"),
        P("tp", None),
        P("tm", "tp"),
        P(None, "tp"),
        P("tm"),
        P("tm"),
        P("tm"),
        P(None, "tp"),
    )
    return jax.shard_map(
        local, mesh=mesh, in_specs=placed, out_specs=P("tm", "tp"), check_vma=False
    )
```

```python
import jax
import jax.numpy as jnp
from jax import lax
from jax.experimental import pallas as pl
from jax.experimental.pallas import tpu as pltpu
from jax.sharding import PartitionSpec as P

HD = 128
WMAX = 4
EPS = 1e-06
FEW = -1e30
MANY = 1e30
LOG2E = 1.4426950408889634
MESH = pl.DeviceIdType.MESH
F32 = jnp.float32
BF16 = jnp.bfloat16


def kernel(
    spans,
    q_hbm,
    k_hbm,
    v_hbm,
    q_gain_ref,
    k_gain_ref,
    w_hbm,
    res_hbm,
    gate_ref,
    fresh_hbm,
    step_ref,
    reach_ref,
    pos_ref,
    out_ref,
    q_own,
    k_own,
    v_own,
    vt_own,
    qn,
    kn,
    qa,
    qb,
    k1,
    vt1,
    k2,
    vt2,
    est,
    st_own,
    st_in,
    os_out,
    os_stat,
    os_in,
    os_in_stat,
    far_out,
    far_stat,
    far_in,
    far_in_stat,
    acc,
    top,
    ag,
    wbuf,
    res,
    total,
    gain_buf,
    fresh,
    load_sem,
    wload_sem,
    fresh_sem,
    est_s,
    est_r,
    st_s,
    st_r,
    q_s,
    q_r,
    qf_s,
    qf_r,
    k_s,
    k_r,
    v_s,
    v_r,
    kf_s,
    kf_r,
    vf_s,
    vf_r,
    os_s,
    os_r,
    oss_s,
    oss_r,
    far_s,
    far_r,
    fars_s,
    fars_r,
    res_s,
    res_r,
    wsib_s,
    wsib_r,
    wx_s,
    wx_r,
    wy_s,
    wy_r,
    ag_s,
    ag_r,
    wz_s,
    gate_sem,
):
    heads, rows = q_own.shape[0], q_own.shape[1]
    local = heads * HD
    width = 4 * local
    out_cols = out_ref.shape[1]
    half_cols = out_cols // 2
    tm = lax.axis_index("tm")
    tp = lax.axis_index("tp")
    lo, core = tp // 2, tp % 2
    x_hi, y, z = (tm // 8) % 2, tm // 16, tm % 8

    def shifted(by):
        return (lax.rem(tm + by + spans, spans), tp)

    peers = [(tm, lax.rem(tp + by, 4)) for by in (1, 2, 3)]
    across = [(tm + 8 - 16 * x_hi, (1 - lo) * 2 + c) for c in (0, 1)]
    turn = jnp.where(z >= 4, 16, -16)
    y_next, y_prev = shifted(turn), shifted(-turn)
    turn_y = turn // 16

    def load(src, dst, slot, h):
        return pltpu.make_async_copy(
            src.at[:, pl.ds(pl.multiple_of(h * HD, HD), HD)], dst.at[h], load_sem.at[slot, h]
        )

    loads = [(q_hbm, q_own, 0), (k_hbm, k_own, 1), (v_hbm, v_own, 2)]
    for src, dst, slot in loads:
        for h in range(heads):
            load(src, dst, slot, h).start()

    first, last = z == 0, z == 7
    edge = jnp.logical_or(first, last)
    inner = jnp.logical_not(edge)
    opposite = [(y * 16 + (i // 4) * 8 + 7 - z, i % 4) for i in range(8)]
    barrier = pltpu.get_barrier_semaphore()
    greet = [shifted(1), shifted(-1), shifted(2), shifted(-2)] + peers + across + [y_prev]
    for other in greet:
        pl.semaphore_signal(barrier, inc=1, device_id=other, device_id_type=MESH)

    @pl.when(edge)
    def _():
        for other in opposite:
            pl.semaphore_signal(barrier, inc=1, device_id=other, device_id_type=MESH)

    w_own_copy = pltpu.make_async_copy(
        w_hbm.at[:, :, pl.ds(pl.multiple_of(tp * out_cols, HD), out_cols)],
        wbuf.at[:, pl.ds(pl.multiple_of(tp * HD, HD), HD), :],
        wload_sem,
    )
    w_own_copy.start()
    fresh_copy = pltpu.make_async_copy(fresh_hbm, fresh, fresh_sem)
    fresh_copy.start()

    ones = jnp.ones((16, rows), BF16)
    for h in range(heads):
        both = q_gain_ref[h * HD : (h + 1) * HD] * k_gain_ref[h * HD : (h + 1) * HD]
        gain_buf[h] = both * (HD ** (-0.5) * LOG2E)
        vt_own[h, HD : HD + 16, :] = ones
        vt1[h, HD : HD + 16, :] = ones
        vt2[h, HD : HD + 16, :] = ones

    def energy_of(ref):
        squares = jnp.zeros((rows, HD), F32)
        for h in range(heads):
            wide = ref[h].astype(F32)
            squares = squares + wide * wide
        return jnp.sum(jnp.transpose(squares), axis=0, keepdims=True)

    for src, dst, slot in loads:
        for h in range(heads):
            load(src, dst, slot, h).wait()
    pl.semaphore_wait(barrier, len(greet) + len(opposite) * edge.astype(jnp.int32))

    def remote(src, dst, send, recv, to):
        return pltpu.make_async_remote_copy(
            src_ref=src, dst_ref=dst, send_sem=send, recv_sem=recv, device_id=to, device_id_type=MESH
        )

    up, down = shifted(1), shifted(-1)
    est_copies = [
        remote(est.at[tp], est.at[tp], est_s.at[i], est_r.at[tp], to) for i, to in enumerate(peers)
    ]

    def est_in(i):
        who = lax.rem(tp + i + 1, 4)
        return remote(est.at[who], est.at[who], est_s.at[i], est_r.at[who], peers[i])

    def q_copy(h):
        return remote(q_own.at[h], qa.at[h], q_s.at[h], q_r.at[h], up)

    def q_forward(h):
        return remote(qa.at[h], qb.at[h], qf_s.at[h], qf_r.at[h], up)

    def k_copy(h):
        return remote(k_own.at[h], k1.at[h], k_s.at[h], k_r.at[h], down)

    def v_copy(h):
        return remote(
            vt_own.at[h, pl.ds(0, HD), :], vt1.at[h, pl.ds(0, HD), :], v_s.at[h], v_r.at[h], down
        )

    def k_forward(h):
        return remote(k1.at[h], k2.at[h], kf_s.at[h], kf_r.at[h], down)

    def v_forward(h):
        return remote(
            vt1.at[h, pl.ds(0, HD), :], vt2.at[h, pl.ds(0, HD), :], vf_s.at[h], vf_r.at[h], down
        )

    def os_copy(h):
        return remote(os_out.at[h], os_in.at[h], os_s.at[h], os_r.at[h], up)

    def os_stat_copy(h):
        return remote(os_stat.at[h], os_in_stat.at[h], oss_s.at[h], oss_r.at[h], up)

    def far_copy(h):
        return remote(far_out.at[h], far_in.at[h], far_s.at[h], far_r.at[h], down)

    def far_stat_copy(h):
        return remote(far_stat.at[h], far_in_stat.at[h], fars_s.at[h], fars_r.at[h], down)

    parts = res_s.shape[0]
    part_rows = rows // parts

    def res_copy(i):
        cut = pl.ds(i * part_rows, part_rows)
        return remote(res_hbm.at[cut], res.at[cut], res_s.at[i], res_r.at[i], up)

    def st_copy(i, by):
        return remote(st_own, st_in.at[i], st_s.at[i], st_r.at[i], shifted(by))

    sibling = (tm, lo * 2 + 1 - core)

    def w_slot(h, who, half):
        return wbuf.at[
            h,
            pl.ds(pl.multiple_of(who * HD, HD), HD),
            pl.ds(pl.multiple_of(half * half_cols, HD), half_cols),
        ]

    def w_sibling():
        return remote(
            w_hbm.at[:, :, pl.ds(pl.multiple_of(sibling[1] * out_cols, HD), out_cols)],
            wbuf.at[:, pl.ds(pl.multiple_of(tp * HD, HD), HD), :],
            wsib_s,
            wsib_r,
            sibling,
        )

    def w_across(c, h):
        column = across[c][1] * out_cols + lax.rem(y, 2) * half_cols
        return remote(
            w_hbm.at[h, :, pl.ds(pl.multiple_of(column, HD), half_cols)],
            w_slot(h, tp, lax.rem(y, 2)),
            wx_s.at[c, h],
            wx_r.at[h],
            across[c],
        )

    def w_piece(piece, h):
        return w_slot(h, (1 - lo) * 2 + piece // 2, lax.rem(piece, 2))

    def w_across_in(h):
        slot = w_piece(y, h)
        return remote(slot, slot, wx_s.at[0, h], wx_r.at[h], across[0])

    def w_outward(h, to):
        slot = w_piece(y, h)
        return remote(slot, slot, wz_s.at[h], wx_r.at[h], to)

    def w_along(k, h):
        slot = w_piece(lax.rem(y - turn_y * k + 4, 4), h)
        return remote(slot, slot, wy_s.at[k, h], wy_r.at[k, h], y_next)

    def w_along_in(k, h):
        slot = w_piece(lax.rem(y - turn_y * (k + 1) + 8, 4), h)
        return remote(slot, slot, wy_s.at[k, h], wy_r.at[k, h], y_next)

    def ag_slot(h, who):
        return ag.at[h, :, pl.ds(pl.multiple_of(who * HD, HD), HD)]

    partner = (tm, (1 - lo) * 2 + core)
    diagonal = (1 - lo) * 2 + 1 - core

    def ag_move(i, h, who, to):
        return remote(ag_slot(h, who), ag_slot(h, who), ag_s.at[i, h], ag_r.at[who, h], to)

    def ag_copies(h):
        return [
            ag_move(0, h, tp, partner),
            ag_move(1, h, tp, sibling),
            ag_move(2, h, partner[1], sibling),
        ]

    def each(body):
        @pl.loop(0, heads)
        def _(h):
            body(h)

    def begin_up():
        @pl.loop(0, heads)
        def _(h):
            q_copy(h).start()

    def begin_keys():
        for h in range(2):
            k_copy(h).start()

    def begin_values():
        for h in range(heads):
            if h >= 2:
                k_copy(h).start()
            v_copy(h).start()

    pl.when(jnp.logical_not(last))(begin_up)
    pl.when(jnp.logical_not(first))(begin_keys)

    @pl.when(jnp.logical_and(core == y // 2, inner))
    def _():
        @pl.loop(0, heads)
        def _(h):
            w_across(0, h).start()
            w_across(1, h).start()

    energy_q = energy_of(q_own)
    energy_k = energy_of(k_own)
    line = lax.broadcasted_iota(jnp.int32, (8, rows), 0)
    message = jnp.where(line == 0, energy_q, 0.0)
    message = jnp.where(line == 1, energy_k, message)
    message = jnp.where(line == 2, reach_ref[0].astype(F32) * 0.25, message)
    message = jnp.where(line == 3, step_ref[0].astype(F32) * 0.25, message)
    est[tp] = message
    for copy in est_copies:
        copy.start()
    for h in range(heads):
        vt_own[h, :HD, :] = jnp.transpose(v_own[h])
    pl.when(jnp.logical_not(first))(begin_values)
    for i in range(3):
        est_in(i).wait_recv()
    st_own[...] = est[0] + est[1] + est[2] + est[3]
    st_moves = [(0, 1), (1, 2), (2, -1), (3, -2)]
    for i, by in st_moves:
        st_copy(i, by).start()


    @pl.when(edge)
    def _():
        for other in opposite:
            pl.semaphore_signal(gate_sem, inc=1, device_id=other, device_id_type=MESH)
        pl.semaphore_wait(gate_sem, len(opposite))

    pl.when(last)(begin_up)

    @pl.when(first)
    def _():
        begin_keys()
        begin_values()

    w_sibling().start()
    def begin_residual():
        for i in range(parts // 2):
            res_copy(i).start()

    def pass_weights():
        @pl.loop(0, heads)
        def _(h):
            w_across_in(h).wait_recv()
            w_along(0, h).start()

            @pl.when(z == 1)
            def _():
                w_outward(h, down).start()

            @pl.when(z == 6)
            def _():
                w_outward(h, up).start()

    pl.when(z == 6)(pass_weights)
    pl.when(z != 6)(begin_residual)

    def column(state, row):
        scale = lax.rsqrt(state[row : row + 1, :] / width + EPS)
        return jnp.transpose(jnp.broadcast_to(scale, (HD, rows)))

    def unit_q(raw, scale, h):
        return (raw.astype(F32) * scale * gain_buf[pl.ds(h, 1), :]).astype(BF16)

    def unit_k(raw, scale):
        return (raw.astype(F32) * scale).astype(BF16)

    def scores_of(keys, queries):
        return lax.dot_general(
            keys, queries, (((1,), (1,)), ((), ())), preferred_element_type=F32
        )

    def alone(keys, queries, values):
        scores = scores_of(keys, queries)
        peak = jnp.max(scores, axis=0, keepdims=True)
        weight = jnp.exp2(scores - peak).astype(BF16)
        return jnp.dot(values, weight, preferred_element_type=F32), peak

    line_8 = lax.broadcasted_iota(jnp.int32, (8, rows), 0)

    def pair(first, second):
        return jnp.where(line_8 == 0, first, second)

    q_scale = column(st_own, 0)
    k_scale = column(st_own, 1)

    def self_part(h):
        q_copy(h).wait_recv()
        q_forward(h).start()
        kn[h] = unit_k(k_own[h], k_scale)
        mixed, peak = alone(kn[h], unit_q(q_own[h], q_scale, h), vt_own[h])
        os_out[h] = mixed[:HD].astype(BF16)
        os_stat[h] = pair(peak, mixed[HD : HD + 1])
        os_copy(h).start()
        os_stat_copy(h).start()

    each(self_part)
    for i in range(parts // 2, parts):
        res_copy(i).start()

    pl.when(z == 6)(begin_residual)
    pl.when(jnp.logical_and(inner, z != 6))(pass_weights)

    st_copy(0, 1).wait_recv()
    state_a = st_in.at[0]
    reach = state_a[2:3, :]
    step = state_a[3:4, :1]
    place = lax.rem(pos_ref[0] + spans - 1, spans)

    def live(distance):
        inside = (place + distance <= spans - 1).astype(F32)
        return jnp.logical_and(reach >= distance, inside > 0.5)

    qa_scale = column(state_a, 0)

    def near_part(h):
        qn[h] = unit_q(qa[h], qa_scale, h)
        scores = scores_of(kn[h], qn[h])
        allowed = live(1)
        peak = jnp.max(scores, axis=0, keepdims=True)
        weight = jnp.exp2(scores - jnp.where(allowed, peak, MANY)).astype(BF16)
        acc[h] = jnp.dot(vt_own[h], weight, preferred_element_type=F32)
        top[h] = jnp.broadcast_to(jnp.where(allowed, peak, FEW), (8, rows))

    each(near_part)

    def join(h, keys, values, allowed):
        scores = scores_of(keys, qn[h])
        before = top[h][:1]
        peak = jnp.where(allowed, jnp.max(scores, axis=0, keepdims=True), FEW)
        after = jnp.maximum(before, peak)
        weight = jnp.exp2(scores - jnp.where(allowed, after, MANY)).astype(BF16)
        acc[h] = acc[h] * jnp.exp2(before - after) + jnp.dot(
            values, weight, preferred_element_type=F32
        )
        top[h] = jnp.broadcast_to(after, (8, rows))

    st_copy(2, -1).wait_recv()
    k1_scale = column(st_in.at[2], 1)

    def second_part(h):
        k_copy(h).wait_recv()
        k_forward(h).start()
        v_copy(h).wait_recv()
        v_forward(h).start()
        join(h, unit_k(k1[h], k1_scale), vt1[h], live(2))

        @pl.when(edge)
        def _():
            w_across_in(h).wait_recv()
            w_along(0, h).start()

    each(second_part)

    st_copy(1, 2).wait_recv()
    st_copy(3, -2).wait_recv()
    qb_scale = column(st_in.at[1], 0)
    k2_scale = column(st_in.at[3], 1)

    def third_part(h):
        q_forward(h).wait_recv()
        k_forward(h).wait_recv()
        v_forward(h).wait_recv()
        keys = unit_k(k2[h], k2_scale)
        mixed, peak = alone(keys, unit_q(qb[h], qb_scale, h), vt2[h])
        far_out[h] = mixed[:HD].astype(BF16)
        far_stat[h] = pair(peak, mixed[HD : HD + 1])
        far_copy(h).start()
        far_stat_copy(h).start()
        join(h, keys, vt2[h], live(3))
        w_along_in(0, h).wait_recv()
        w_along(1, h).start()

        @pl.when(h > 0)
        def _():
            w_along_in(1, h - 1).wait_recv()
            w_along(2, h - 1).start()

    each(third_part)
    w_along_in(1, heads - 1).wait_recv()
    w_along(2, heads - 1).start()

    def project(h):
        ag_move(0, h, sibling[1], sibling).wait_recv()
        ag_move(0, h, diagonal, sibling).wait_recv()
        w_along_in(2, h).wait_recv()

        @pl.loop(0, out_cols // 256)
        def _(j):
            cut = pl.ds(pl.multiple_of(j * 256, 256), 256)
            fresh = jnp.dot(ag[h], wbuf[h, :, cut], preferred_element_type=F32)
            total[:, cut] = total[:, cut] + fresh

    total[...] = jnp.zeros_like(total)

    def merge(h):
        os_copy(h).wait_recv()
        os_stat_copy(h).wait_recv()
        far_copy(h).wait_recv()
        far_stat_copy(h).wait_recv()
        state_s, state_f = os_in_stat[h], far_in_stat[h]
        peak_s, peak_m = state_s[:1], top[h][:1]
        peak_f = jnp.where(live(4), state_f[:1], FEW)
        peak = jnp.maximum(jnp.maximum(peak_s, peak_m), peak_f)
        by_s, by_m, by_f = jnp.exp2(peak_s - peak), jnp.exp2(peak_m - peak), jnp.exp2(peak_f - peak)
        mixed = acc[h]
        whole = state_s[1:2] * by_s + mixed[HD : HD + 1] * by_m + state_f[1:2] * by_f
        share = 1.0 / whole
        attended = (
            os_in[h].astype(F32) * (by_s * share)
            + mixed[:HD] * (by_m * share)
            + far_in[h].astype(F32) * (by_f * share)
        )
        ag[h, :, pl.ds(pl.multiple_of(tp * HD, HD), HD)] = jnp.transpose(attended).astype(BF16)
        for copy in ag_copies(h)[:2]:
            copy.start()

    def relay(h):
        ag_move(0, h, partner[1], partner).wait_recv()
        ag_copies(h)[2].start()

    merge(0)
    w_own_copy.wait()
    w_sibling().wait_recv()

    merge(1)
    relay(0)

    @pl.loop(2, heads)
    def _(h):
        merge(h)
        relay(h - 1)
        project(h - 2)

    relay(heads - 1)
    project(heads - 2)
    project(heads - 1)
    for i in range(parts):
        res_copy(i).wait_recv()
    table = gate_ref[...].astype(F32)
    pick = lax.broadcasted_iota(jnp.int32, table.shape, 0).astype(F32) == step
    gate = jnp.sum(jnp.where(pick, table, 0.0), axis=0, keepdims=True)
    fresh_copy.wait()
    updated = (res[...].astype(F32) + gate * total[...]).astype(BF16)
    newest = jnp.full(updated.shape, pos_ref[0], jnp.int32) == 0
    out_ref[...] = jnp.where(newest, fresh[...], updated)

    for copy in est_copies:
        copy.wait_send()
    for i, by in st_moves:
        st_copy(i, by).wait_send()
    for i in range(parts):
        res_copy(i).wait_send()
    w_sibling().wait_send()

    @pl.when(jnp.logical_and(core == y // 2, inner))
    def _():
        @pl.loop(0, heads)
        def _(h):
            w_across(0, h).wait_send()
            w_across(1, h).wait_send()

    @pl.when(jnp.logical_or(z == 1, z == 6))
    def _():
        @pl.loop(0, heads)
        def _(h):
            w_outward(h, down).wait_send()

    def sent(h):
        for copy in (
            q_copy,
            q_forward,
            k_copy,
            v_copy,
            k_forward,
            v_forward,
            os_copy,
            os_stat_copy,
            far_copy,
            far_stat_copy,
        ):
            copy(h).wait_send()
        for i in range(3):
            w_along(i, h).wait_send()
        for copy in ag_copies(h):
            copy.wait_send()

    each(sent)


def local(
    queries,
    key_rows,
    value_rows,
    query_gain,
    key_gain,
    out_weight,
    residual,
    gate_table,
    timesteps,
    windows,
    queue_positions,
    fresh_span,
):
    spans = lax.axis_size("tm")
    rows, width = queries.shape
    heads = width // HD
    out_cols = residual.shape[1]
    weight = out_weight.reshape(heads, HD, out_weight.shape[1])
    chunk = pltpu.VMEM((heads, rows, HD), BF16)
    flat = pltpu.VMEM((heads, HD, rows), BF16)
    tall = pltpu.VMEM((heads, HD + 16, rows), BF16)
    stats = pltpu.VMEM((heads, 8, rows), F32)
    one = pltpu.SemaphoreType.DMA
    per_head = one((heads,))
    parts = 4
    hbm = pl.BlockSpec(memory_space=pl.ANY)
    vmem = pl.BlockSpec(memory_space=pltpu.VMEM)
    smem = pl.BlockSpec(memory_space=pltpu.SMEM)

    def run(*operands):
        def body(*refs):
            kernel(spans, *refs)

        return pl.pallas_call(
            body,
            out_shape=jax.ShapeDtypeStruct((rows, out_cols), BF16),
            in_specs=[hbm, hbm, hbm, vmem, vmem, hbm, hbm, vmem, hbm, smem, smem, smem],
            out_specs=vmem,
            scratch_shapes=[
                chunk,
                chunk,
                chunk,
                tall,
                chunk,
                chunk,
                chunk,
                chunk,
                chunk,
                tall,
                chunk,
                tall,
                pltpu.VMEM((4, 8, rows), F32),
                pltpu.VMEM((8, rows), F32),
                pltpu.VMEM((4, 8, rows), F32),
                flat,
                stats,
                flat,
                stats,
                flat,
                stats,
                flat,
                stats,
                pltpu.VMEM((heads, HD + 16, rows), F32),
                stats,
                pltpu.VMEM((heads, rows, 4 * HD), BF16),
                pltpu.VMEM((heads, 4 * HD, out_cols), BF16),
                pltpu.VMEM((rows, out_cols), BF16),
                pltpu.VMEM((rows, out_cols), F32),
                pltpu.VMEM((heads, HD), F32),
                pltpu.VMEM((rows, out_cols), BF16),
                one((3, heads)),
                one,
                one,
                one((3,)),
                one((4,)),
                one((4,)),
                one((4,)),
                per_head,
                per_head,
                per_head,
                per_head,
                per_head,
                per_head,
                per_head,
                per_head,
                per_head,
                per_head,
                per_head,
                per_head,
                per_head,
                per_head,
                per_head,
                per_head,
                per_head,
                per_head,
                per_head,
                per_head,
                one((parts,)),
                one((parts,)),
                one,
                one,
                one((2, heads)),
                per_head,
                one((3, heads)),
                one((3, heads)),
                one((3, heads)),
                one((4, heads)),
                per_head,
                pltpu.SemaphoreType.REGULAR,
            ],
            compiler_params=pltpu.CompilerParams(
                collective_id=0, has_side_effects=True, vmem_limit_bytes=56 * 2**20
            ),
            name="window_block",
        )(*operands)

    return run(
        queries,
        key_rows,
        value_rows,
        query_gain,
        key_gain,
        weight,
        residual,
        gate_table,
        fresh_span,
        timesteps,
        windows,
        queue_positions,
    )


def solution(mesh):
    placed = (
        P("tm", "tp"),
        P("tm", "tp"),
        P("tm", "tp"),
        P("tp"),
        P("tp"),
        P("tp", None),
        P("tm", "tp"),
        P(None, "tp"),
        P("tm"),
        P("tm"),
        P("tm"),
        P(None, "tp"),
    )
    return jax.shard_map(
        local, mesh=mesh, in_specs=placed, out_specs=P("tm", "tp"), check_vma=False
    )
```

```python
import jax
import jax.numpy as jnp
from jax import lax
from jax.experimental import pallas as pl
from jax.experimental.pallas import tpu as pltpu
from jax.sharding import PartitionSpec as P

HD = 128
WMAX = 4
EPS = 1e-06
FEW = -1e30
MANY = 1e30
LOG2E = 1.4426950408889634
MESH = pl.DeviceIdType.MESH
F32 = jnp.float32
BF16 = jnp.bfloat16


def kernel(
    spans,
    q_hbm,
    k_hbm,
    v_hbm,
    q_gain_ref,
    k_gain_ref,
    w_hbm,
    res_hbm,
    gate_ref,
    fresh_hbm,
    step_ref,
    reach_ref,
    pos_ref,
    out_ref,
    q_own,
    k_own,
    v_own,
    vt_own,
    qn,
    kn,
    qa,
    qb,
    k1,
    vt1,
    k2,
    vt2,
    est,
    st_own,
    st_in,
    os_out,
    os_stat,
    os_in,
    os_in_stat,
    far_out,
    far_stat,
    far_in,
    far_in_stat,
    acc,
    top,
    ag,
    wbuf,
    res,
    total,
    gain_buf,
    gate_buf,
    fresh,
    load_sem,
    wload_sem,
    fresh_sem,
    est_s,
    est_r,
    st_s,
    st_r,
    q_s,
    q_r,
    qf_s,
    qf_r,
    k_s,
    k_r,
    v_s,
    v_r,
    kf_s,
    kf_r,
    vf_s,
    vf_r,
    os_s,
    os_r,
    oss_s,
    oss_r,
    far_s,
    far_r,
    fars_s,
    fars_r,
    res_s,
    res_r,
    wsib_s,
    wsib_r,
    wx_s,
    wx_r,
    wy_s,
    wy_r,
    ag_s,
    ag_r,
    wz_s,
    wz_r,
    gate_sem,
):
    heads, rows = q_own.shape[0], q_own.shape[1]
    local = heads * HD
    width = 4 * local
    out_cols = out_ref.shape[1]
    strip, half, sideways = HD // 4, HD // 8, 3
    tm = lax.axis_index("tm")
    tp = lax.axis_index("tp")
    lo, core = tp // 2, tp % 2
    x_hi, y, z = (tm // 8) % 2, tm // 16, tm % 8

    def shifted(by):
        return (lax.rem(tm + by + spans, spans), tp)

    peers = [(tm, lax.rem(tp + by, 4)) for by in (1, 2, 3)]
    across = [(tm + 8 - 16 * x_hi, (1 - lo) * 2 + c) for c in (0, 1)]
    sides = [[(tm, (1 - lo) * 2 + c) for c in (0, 1)], across]
    turn = jnp.where(z >= 4, 16, -16)
    y_next, y_prev = shifted(turn), shifted(-turn)
    turn_y = turn // 16

    def load(src, dst, slot, h):
        return pltpu.make_async_copy(
            src.at[:, pl.ds(pl.multiple_of(h * HD, HD), HD)], dst.at[h], load_sem.at[slot, h]
        )

    loads = [(q_hbm, q_own, 0), (k_hbm, k_own, 1), (v_hbm, v_own, 2)]
    for src, dst, slot in loads:
        for h in range(heads):
            load(src, dst, slot, h).start()

    first, last = z == 0, z == 7
    edge = jnp.logical_or(first, last)
    inner = jnp.logical_not(edge)
    opposite = [(y * 16 + (i // 4) * 8 + 7 - z, i % 4) for i in range(8)]
    barrier = pltpu.get_barrier_semaphore()
    greet = [shifted(1), shifted(-1), shifted(2), shifted(-2)] + peers + across + [y_prev]
    for other in greet:
        pl.semaphore_signal(barrier, inc=1, device_id=other, device_id_type=MESH)

    @pl.when(edge)
    def _():
        for other in opposite:
            pl.semaphore_signal(barrier, inc=1, device_id=other, device_id_type=MESH)

    w_own_copy = pltpu.make_async_copy(
        w_hbm.at[:, :, pl.ds(pl.multiple_of(tp * out_cols, HD), out_cols)],
        wbuf.at[:, tp],
        wload_sem,
    )
    w_own_copy.start()
    fresh_copy = pltpu.make_async_copy(fresh_hbm, fresh, fresh_sem)
    fresh_copy.start()

    def energy_of(ref):
        squares = jnp.zeros((rows, HD), F32)
        for h in range(heads):
            wide = ref[h].astype(F32)
            squares = squares + wide * wide
        return jnp.sum(jnp.transpose(squares), axis=0, keepdims=True)

    for src, dst, slot in loads[:2]:
        for h in range(heads):
            load(src, dst, slot, h).wait()
    energy_q = energy_of(q_own)
    energy_k = energy_of(k_own)
    line = lax.broadcasted_iota(jnp.int32, (8, rows), 0)
    message = jnp.where(line == 0, energy_q, 0.0)
    message = jnp.where(line == 1, energy_k, message)
    message = jnp.where(line == 2, reach_ref[0].astype(F32) * 0.25, message)
    message = jnp.where(line == 3, step_ref[0].astype(F32) * 0.25, message)
    est[tp] = message
    pl.semaphore_wait(barrier, len(greet) + len(opposite) * edge.astype(jnp.int32))

    def remote(src, dst, send, recv, to):
        return pltpu.make_async_remote_copy(
            src_ref=src, dst_ref=dst, send_sem=send, recv_sem=recv, device_id=to, device_id_type=MESH
        )

    up, down = shifted(1), shifted(-1)
    est_copies = [
        remote(est.at[tp], est.at[tp], est_s.at[i], est_r.at[tp], to) for i, to in enumerate(peers)
    ]

    def est_in(i):
        who = lax.rem(tp + i + 1, 4)
        return remote(est.at[who], est.at[who], est_s.at[i], est_r.at[who], peers[i])

    def q_copy(h):
        return remote(q_own.at[h], qa.at[h], q_s.at[h], q_r.at[h], up)

    def q_forward(h):
        return remote(qa.at[h], qb.at[h], qf_s.at[h], qf_r.at[h], up)

    def k_copy(h):
        return remote(k_own.at[h], k1.at[h], k_s.at[h], k_r.at[h], down)

    def v_copy(h):
        return remote(
            vt_own.at[h, pl.ds(0, HD), :], vt1.at[h, pl.ds(0, HD), :], v_s.at[h], v_r.at[h], down
        )

    def k_forward(h):
        return remote(k1.at[h], k2.at[h], kf_s.at[h], kf_r.at[h], down)

    def v_forward(h):
        return remote(
            vt1.at[h, pl.ds(0, HD), :], vt2.at[h, pl.ds(0, HD), :], vf_s.at[h], vf_r.at[h], down
        )

    def os_copy(h):
        return remote(os_out.at[h], os_in.at[h], os_s.at[h], os_r.at[h], up)

    def os_stat_copy(h):
        return remote(os_stat.at[h], os_in_stat.at[h], oss_s.at[h], oss_r.at[h], up)

    def far_copy(h):
        return remote(far_out.at[h], far_in.at[h], far_s.at[h], far_r.at[h], down)

    def far_stat_copy(h):
        return remote(far_stat.at[h], far_in_stat.at[h], fars_s.at[h], fars_r.at[h], down)

    parts = res_s.shape[0]
    part_rows = rows // parts

    def res_copy(i):
        cut = pl.ds(i * part_rows, part_rows)
        return remote(res_hbm.at[cut], res.at[cut], res_s.at[i], res_r.at[i], up)

    def st_copy(i, by):
        return remote(st_own, st_in.at[i], st_s.at[i], st_r.at[i], shifted(by))

    sibling = (tm, lo * 2 + 1 - core)

    def w_sibling():
        return remote(
            w_hbm.at[:, :, pl.ds(pl.multiple_of(sibling[1] * out_cols, HD), out_cols)],
            wbuf.at[:, tp],
            wsib_s,
            wsib_r,
            sibling,
        )

    def piece_rows(piece):
        return pl.ds(pl.multiple_of(piece * strip, strip), strip)

    def w_rows(side):
        return pl.ds(pl.multiple_of(y * strip + side * half, half), half)

    def w_import(side, c, part, some):
        to = sides[side][c]
        these = pl.ds(0, some)
        return remote(
            w_hbm.at[
                these, w_rows(part), pl.ds(pl.multiple_of(to[1] * out_cols, HD), out_cols)
            ],
            wbuf.at[these, tp, w_rows(part), :],
            wx_s.at[side, c],
            wx_r.at[side, core],
            to,
        )

    def w_import_in(side, c, part, some):
        slot = wbuf.at[pl.ds(0, some), (1 - lo) * 2 + c, w_rows(part), :]
        return remote(slot, slot, wx_s.at[side, c], wx_r.at[side, c], sides[side][c])

    def w_exports(act):
        @pl.when(inner)
        def _():
            for side in (0, 1):
                for c in (0, 1):
                    act(w_import(side, c, side, heads))

        for side in (0, 1):

            @pl.when(jnp.logical_and(edge, core == side))
            def _():
                for c in (0, 1):
                    act(w_import(side, c, 0, sideways))

    def w_piece(piece, h):
        return wbuf.at[h, pl.ds((1 - lo) * 2, 2), piece_rows(piece), :]

    def w_outward(h, to, rows_there):
        slot = wbuf.at[h, pl.ds((1 - lo) * 2, 2), rows_there, :]
        return remote(slot, slot, wz_s.at[h], wz_r.at[h], to)

    def outward(h, to, act):
        @pl.when(h < sideways)
        def _():
            act(w_outward(h, to, w_rows(1)))

        @pl.when(h >= sideways)
        def _():
            act(w_outward(h, to, piece_rows(y)))

    def w_along(k, h):
        slot = w_piece(lax.rem(y - turn_y * k + 4, 4), h)
        return remote(slot, slot, wy_s.at[k, h], wy_r.at[k, h], y_next)

    def w_along_in(k, h):
        slot = w_piece(lax.rem(y - turn_y * (k + 1) + 8, 4), h)
        return remote(slot, slot, wy_s.at[k, h], wy_r.at[k, h], y_next)

    half_rows = rows // 2

    def ag_slot(h, who, cut):
        return ag.at[h, who, cut]

    def unit(u):
        if isinstance(u, int) and u >= heads - 1:
            return heads - 1, pl.ds((u - heads + 1) * half_rows, half_rows)
        return u, pl.ds(0, rows)

    partner = (tm, (1 - lo) * 2 + core)
    diagonal = (1 - lo) * 2 + 1 - core

    def ag_move(i, u, who, to):
        h, cut = unit(u)
        slot = ag_slot(h, who, cut)
        return remote(slot, slot, ag_s.at[i, u], ag_r.at[who, u], to)

    def ag_copies(u):
        return [
            ag_move(0, u, tp, partner),
            ag_move(1, u, tp, sibling),
            ag_move(2, u, partner[1], sibling),
        ]

    def each(body):
        @pl.loop(0, heads)
        def _(h):
            body(h)

    def begin_up(some, end):
        @pl.loop(some, end)
        def _(h):
            q_copy(h).start()

    def begin_keys():
        for h in range(early):
            k_copy(h).start()

    def begin_values():
        for h in range(early):
            v_copy(h).start()

    def begin_rest():
        @pl.loop(early, heads)
        def _(h):
            k_copy(h).start()
            v_copy(h).start()

    early = 2
    for copy in est_copies:
        copy.start()
    pl.when(jnp.logical_not(first))(begin_keys)

    @pl.when(jnp.logical_not(last))
    def _():
        begin_up(0, early)

    w_exports(lambda copy: copy.start())

    ones = jnp.ones((16, rows), BF16)
    for h in range(heads):
        load(v_hbm, v_own, 2, h).wait()
        vt_own[h, :HD, :] = jnp.transpose(v_own[h])
        vt_own[h, HD : HD + 16, :] = ones
        if h == early - 1:
            pl.when(jnp.logical_not(first))(begin_values)

    for i in range(3):
        est_in(i).wait_recv()
    st_own[...] = est[0] + est[1] + est[2] + est[3]
    st_moves = [(0, 1), (1, 2), (2, -1), (3, -2)]
    for i, by in st_moves:
        st_copy(i, by).start()

    @pl.when(jnp.logical_not(last))
    def _():
        begin_up(early, heads)

    pl.when(jnp.logical_not(first))(begin_rest)
    for h in range(heads):
        both = q_gain_ref[h * HD : (h + 1) * HD] * k_gain_ref[h * HD : (h + 1) * HD]
        gain_buf[h] = both * (HD ** (-0.5) * LOG2E)
        vt1[h, HD : HD + 16, :] = ones
        vt2[h, HD : HD + 16, :] = ones

    def pass_weights():
        for side in (0, 1):
            for c in (0, 1):
                w_import_in(side, c, side, heads).wait_recv()

        @pl.loop(0, heads)
        def _(h):
            w_along(0, h).start()

            @pl.when(z == 1)
            def _():
                outward(h, down, lambda copy: copy.start())

            @pl.when(z == 6)
            def _():
                outward(h, up, lambda copy: copy.start())

    pl.when(inner)(pass_weights)

    @pl.when(edge)
    def _():
        for side in (0, 1):
            w_import_in(side, side, 0, sideways).wait_recv()
        for other in opposite:
            pl.semaphore_signal(gate_sem, inc=1, device_id=other, device_id_type=MESH)
        pl.semaphore_wait(gate_sem, len(opposite))

    @pl.when(last)
    def _():
        begin_up(0, heads)

    @pl.when(first)
    def _():
        begin_keys()
        begin_values()
        begin_rest()

    w_sibling().start()
    def begin_residual():
        for i in range(parts // 2):
            res_copy(i).start()

    pl.when(z != 6)(begin_residual)

    def column(state, row):
        scale = lax.rsqrt(state[row : row + 1, :] / width + EPS)
        return jnp.transpose(jnp.broadcast_to(scale, (HD, rows)))

    def unit_q(raw, scale, h):
        return (raw.astype(F32) * scale * gain_buf[pl.ds(h, 1), :]).astype(BF16)

    def unit_k(raw, scale):
        return (raw.astype(F32) * scale).astype(BF16)

    def scores_of(keys, queries):
        return lax.dot_general(
            keys, queries, (((1,), (1,)), ((), ())), preferred_element_type=F32
        )

    def alone(keys, queries, values):
        scores = scores_of(keys, queries)
        peak = jnp.max(scores, axis=0, keepdims=True)
        weight = jnp.exp2(scores - peak).astype(BF16)
        return jnp.dot(values, weight, preferred_element_type=F32), peak

    fold = rows // HD

    def pair(first, second):
        return jnp.concatenate(
            [one[:, i * HD : (i + 1) * HD] for one in (first, second) for i in range(fold)], axis=0
        )

    def unpair(packed):
        first = jnp.concatenate([packed[i : i + 1] for i in range(fold)], axis=1)
        second = jnp.concatenate([packed[fold + i : fold + i + 1] for i in range(fold)], axis=1)
        return first, second

    q_scale = column(st_own, 0)
    k_scale = column(st_own, 1)

    def self_part(h):
        q_copy(h).wait_recv()
        q_forward(h).start()
        kn[h] = unit_k(k_own[h], k_scale)
        mixed, peak = alone(kn[h], unit_q(q_own[h], q_scale, h), vt_own[h])
        os_out[h] = mixed[:HD].astype(BF16)
        os_stat[h] = pair(peak, mixed[HD : HD + 1])
        os_copy(h).start()
        os_stat_copy(h).start()

    each(self_part)
    pl.when(z == 6)(begin_residual)
    for i in range(parts // 2, parts):
        res_copy(i).start()

    st_copy(0, 1).wait_recv()
    state_a = st_in.at[0]
    reach = state_a[2:3, :]
    step = state_a[3:4, :1]
    place = lax.rem(pos_ref[0] + spans - 1, spans)

    def live(distance):
        inside = (place + distance <= spans - 1).astype(F32)
        return jnp.logical_and(reach >= distance, inside > 0.5)

    qa_scale = column(state_a, 0)

    def near_part(h):
        qn[h] = unit_q(qa[h], qa_scale, h)
        scores = scores_of(kn[h], qn[h])
        allowed = live(1)
        peak = jnp.max(scores, axis=0, keepdims=True)
        weight = jnp.exp2(scores - jnp.where(allowed, peak, MANY)).astype(BF16)
        acc[h] = jnp.dot(vt_own[h], weight, preferred_element_type=F32)
        top[h] = jnp.broadcast_to(jnp.where(allowed, peak, FEW), (8, rows))

    each(near_part)

    def join(h, keys, values, allowed):
        scores = scores_of(keys, qn[h])
        before = top[h][:1]
        peak = jnp.where(allowed, jnp.max(scores, axis=0, keepdims=True), FEW)
        after = jnp.maximum(before, peak)
        weight = jnp.exp2(scores - jnp.where(allowed, after, MANY)).astype(BF16)
        acc[h] = acc[h] * jnp.exp2(before - after) + jnp.dot(
            values, weight, preferred_element_type=F32
        )
        top[h] = jnp.broadcast_to(after, (8, rows))

    st_copy(2, -1).wait_recv()
    k1_scale = column(st_in.at[2], 1)

    def second_part(h):
        k_copy(h).wait_recv()
        k_forward(h).start()
        v_copy(h).wait_recv()
        v_forward(h).start()
        join(h, unit_k(k1[h], k1_scale), vt1[h], live(2))

        @pl.when(edge)
        def _():
            outward(h, up, lambda copy: copy.wait_recv())
            w_along(0, h).start()

    each(second_part)

    st_copy(1, 2).wait_recv()
    st_copy(3, -2).wait_recv()
    qb_scale = column(st_in.at[1], 0)
    k2_scale = column(st_in.at[3], 1)

    def third_part(h):
        q_forward(h).wait_recv()
        k_forward(h).wait_recv()
        v_forward(h).wait_recv()
        keys = unit_k(k2[h], k2_scale)
        mixed, peak = alone(keys, unit_q(qb[h], qb_scale, h), vt2[h])
        far_out[h] = mixed[:HD].astype(BF16)
        far_stat[h] = pair(peak, mixed[HD : HD + 1])
        far_copy(h).start()
        far_stat_copy(h).start()
        join(h, keys, vt2[h], live(3))
        w_along_in(0, h).wait_recv()
        w_along(1, h).start()

        @pl.when(h > 0)
        def _():
            w_along_in(1, h - 1).wait_recv()
            w_along(2, h - 1).start()

    each(third_part)
    w_along_in(1, heads - 1).wait_recv()
    w_along(2, heads - 1).start()

    def tiles(body):
        @pl.loop(0, out_cols // 256)
        def _(j):
            body(pl.ds(pl.multiple_of(j * 256, 256), 256))

    def product(h, cut):
        left = jnp.concatenate([ag[h, i] for i in range(4)], axis=1)
        return jnp.dot(left, wbuf[h, :, :, cut].reshape(4 * HD, 256), preferred_element_type=F32)

    def project(h):
        ag_move(0, h, sibling[1], sibling).wait_recv()
        ag_move(0, h, diagonal, sibling).wait_recv()
        w_along_in(2, h).wait_recv()

        def body(cut):
            total[:, cut] = total[:, cut] + product(h, cut)

        tiles(body)

    total[...] = jnp.zeros_like(total)

    def arrived(h):
        os_copy(h).wait_recv()
        os_stat_copy(h).wait_recv()
        far_copy(h).wait_recv()
        far_stat_copy(h).wait_recv()

    def merge(u):
        h, _ = unit(u)
        cut = slice(0, rows)
        if isinstance(u, int) and u >= heads - 1:
            cut = slice((u - heads + 1) * half_rows, (u - heads + 2) * half_rows)
        peak_s, sum_s = (one[:, cut] for one in unpair(os_in_stat[h]))
        peak_f, sum_f = (one[:, cut] for one in unpair(far_in_stat[h]))
        peak_m = top[h, :1, cut]
        peak_f = jnp.where(live(4)[:, cut], peak_f, FEW)
        peak = jnp.maximum(jnp.maximum(peak_s, peak_m), peak_f)
        by_s, by_m, by_f = jnp.exp2(peak_s - peak), jnp.exp2(peak_m - peak), jnp.exp2(peak_f - peak)
        mixed = acc[h, :, cut]
        whole = sum_s * by_s + mixed[HD : HD + 1] * by_m + sum_f * by_f
        share = 1.0 / whole
        attended = (
            os_in[h, :, cut].astype(F32) * (by_s * share)
            + mixed[:HD] * (by_m * share)
            + far_in[h, :, cut].astype(F32) * (by_f * share)
        )
        ag[h, tp, cut] = jnp.transpose(attended).astype(BF16)
        for copy in ag_copies(u)[:2]:
            copy.start()

    def relay(u):
        ag_move(0, u, partner[1], partner).wait_recv()
        ag_copies(u)[2].start()

    w_own_copy.wait()
    w_sibling().wait_recv()
    final = heads - 1
    for h in range(final):
        arrived(h)
        merge(h)
        if h >= 2:
            relay(h - 2)
        if h >= 3:
            project(h - 3)
    arrived(final)
    merge(final)
    merge(final + 1)
    for h in range(final - 2, final):
        relay(h)
        project(h - 1)
    for i in range(parts):
        res_copy(i).wait_recv()
    fresh_copy.wait()
    table = gate_ref[...].astype(F32)
    pick = lax.broadcasted_iota(jnp.int32, table.shape, 0).astype(F32) == step
    gate_buf[...] = jnp.sum(jnp.where(pick, table, 0.0), axis=0, keepdims=True)
    relay(final)
    relay(final + 1)
    project(final - 1)
    w_along_in(2, final).wait_recv()

    for u in (final, final + 1):
        ag_move(0, u, sibling[1], sibling).wait_recv()
        ag_move(0, u, diagonal, sibling).wait_recv()
        part = slice((u - final) * half_rows, (u - final + 1) * half_rows)

        def finish(cut, part=part):
            right = wbuf[final, :, :, cut].reshape(4 * HD, 256)
            left = jnp.concatenate([ag[final, i, part] for i in range(4)], axis=1)
            last_term = jnp.dot(left, right, preferred_element_type=F32)
            projected = total[part, cut] + last_term
            updated = (res[part, cut].astype(F32) + gate_buf[:, cut] * projected).astype(BF16)
            newest = jnp.full(updated.shape, pos_ref[0], jnp.int32) == 0
            out_ref[part, cut] = jnp.where(newest, fresh[part, cut], updated)

        tiles(finish)

    for copy in est_copies:
        copy.wait_send()
    for i, by in st_moves:
        st_copy(i, by).wait_send()
    for i in range(parts):
        res_copy(i).wait_send()
    w_sibling().wait_send()

    w_exports(lambda copy: copy.wait_send())

    @pl.when(jnp.logical_or(z == 1, z == 6))
    def _():
        @pl.loop(0, heads)
        def _(h):
            outward(h, down, lambda copy: copy.wait_send())

    def sent(h):
        for copy in (
            q_copy,
            q_forward,
            k_copy,
            v_copy,
            k_forward,
            v_forward,
            os_copy,
            os_stat_copy,
            far_copy,
            far_stat_copy,
        ):
            copy(h).wait_send()
        for i in range(3):
            w_along(i, h).wait_send()

    each(sent)
    for u in range(heads + 1):
        for copy in ag_copies(u):
            copy.wait_send()


def local(
    queries,
    key_rows,
    value_rows,
    query_gain,
    key_gain,
    out_weight,
    residual,
    gate_table,
    timesteps,
    windows,
    queue_positions,
    fresh_span,
):
    spans = lax.axis_size("tm")
    rows, width = queries.shape
    heads = width // HD
    out_cols = residual.shape[1]
    weight = out_weight.reshape(heads, HD, out_weight.shape[1])
    chunk = pltpu.VMEM((heads, rows, HD), BF16)
    flat = pltpu.VMEM((heads, HD, rows), BF16)
    tall = pltpu.VMEM((heads, HD + 16, rows), BF16)
    stats = pltpu.VMEM((heads, 8, rows), F32)
    packed = pltpu.VMEM((heads, 2 * (rows // HD), HD), F32)
    one = pltpu.SemaphoreType.DMA
    per_head = one((heads,))
    parts = 4
    hbm = pl.BlockSpec(memory_space=pl.ANY)
    vmem = pl.BlockSpec(memory_space=pltpu.VMEM)
    smem = pl.BlockSpec(memory_space=pltpu.SMEM)

    def run(*operands):
        def body(*refs):
            kernel(spans, *refs)

        return pl.pallas_call(
            body,
            out_shape=jax.ShapeDtypeStruct((rows, out_cols), BF16),
            in_specs=[hbm, hbm, hbm, vmem, vmem, hbm, hbm, vmem, hbm, smem, smem, smem],
            out_specs=vmem,
            scratch_shapes=[
                chunk,
                chunk,
                chunk,
                tall,
                chunk,
                chunk,
                chunk,
                chunk,
                chunk,
                tall,
                chunk,
                tall,
                pltpu.VMEM((4, 8, rows), F32),
                pltpu.VMEM((8, rows), F32),
                pltpu.VMEM((4, 8, rows), F32),
                flat,
                packed,
                flat,
                packed,
                flat,
                packed,
                flat,
                packed,
                pltpu.VMEM((heads, HD + 16, rows), F32),
                stats,
                pltpu.VMEM((heads, 4, rows, HD), BF16),
                pltpu.VMEM((heads, 4, HD, out_cols), BF16),
                pltpu.VMEM((rows, out_cols), BF16),
                pltpu.VMEM((rows, out_cols), F32),
                pltpu.VMEM((heads, HD), F32),
                pltpu.VMEM((1, out_cols), F32),
                pltpu.VMEM((rows, out_cols), BF16),
                one((3, heads)),
                one,
                one,
                one((3,)),
                one((4,)),
                one((4,)),
                one((4,)),
                per_head,
                per_head,
                per_head,
                per_head,
                per_head,
                per_head,
                per_head,
                per_head,
                per_head,
                per_head,
                per_head,
                per_head,
                per_head,
                per_head,
                per_head,
                per_head,
                per_head,
                per_head,
                per_head,
                per_head,
                one((parts,)),
                one((parts,)),
                one,
                one,
                one((2, 2)),
                one((2, 2)),
                one((3, heads)),
                one((3, heads)),
                one((3, heads + 1)),
                one((4, heads + 1)),
                per_head,
                per_head,
                pltpu.SemaphoreType.REGULAR,
            ],
            compiler_params=pltpu.CompilerParams(
                collective_id=0, has_side_effects=True, vmem_limit_bytes=56 * 2**20
            ),
            name="window_block",
        )(*operands)

    return run(
        queries,
        key_rows,
        value_rows,
        query_gain,
        key_gain,
        weight,
        residual,
        gate_table,
        fresh_span,
        timesteps,
        windows,
        queue_positions,
    )


def solution(mesh):
    placed = (
        P("tm", "tp"),
        P("tm", "tp"),
        P("tm", "tp"),
        P("tp"),
        P("tp"),
        P("tp", None),
        P("tm", "tp"),
        P(None, "tp"),
        P("tm"),
        P("tm"),
        P("tm"),
        P(None, "tp"),
    )
    return jax.shard_map(
        local, mesh=mesh, in_specs=placed, out_specs=P("tm", "tp"), check_vma=False
    )
```

```python
import jax
import jax.numpy as jnp
from jax import lax
from jax.experimental import pallas as pl
from jax.experimental.pallas import tpu as pltpu
from jax.sharding import PartitionSpec as P

HD = 128
WMAX = 4
EPS = 1e-06
FEW = -1e30
MANY = 1e30
LOG2E = 1.4426950408889634
MESH = pl.DeviceIdType.MESH
F32 = jnp.float32
BF16 = jnp.bfloat16


def kernel(
    spans,
    q_hbm,
    k_hbm,
    v_hbm,
    q_gain_ref,
    k_gain_ref,
    w_hbm,
    res_hbm,
    gate_ref,
    fresh_hbm,
    step_ref,
    reach_ref,
    pos_ref,
    out_ref,
    q_own,
    k_own,
    v_own,
    vt_own,
    qn,
    kn,
    qa,
    qb,
    k1,
    vt1,
    k2,
    vt2,
    est,
    st_own,
    st_in,
    os_out,
    os_stat,
    os_in,
    os_in_stat,
    far_out,
    far_stat,
    far_in,
    far_in_stat,
    acc,
    top,
    ag,
    wbuf,
    res,
    total,
    gain_buf,
    gate_buf,
    fresh,
    load_sem,
    wload_sem,
    fresh_sem,
    est_s,
    est_r,
    st_s,
    st_r,
    q_s,
    q_r,
    qf_s,
    qf_r,
    k_s,
    k_r,
    v_s,
    v_r,
    kf_s,
    kf_r,
    vf_s,
    vf_r,
    os_s,
    os_r,
    oss_s,
    oss_r,
    far_s,
    far_r,
    fars_s,
    fars_r,
    res_s,
    res_r,
    wsib_s,
    wsib_r,
    wx_s,
    wx_r,
    wy_s,
    wy_r,
    ag_s,
    ag_r,
    wz_s,
    wz_r,
    gate_sem,
):
    heads, rows = q_own.shape[0], q_own.shape[1]
    local = heads * HD
    width = 4 * local
    out_cols = out_ref.shape[1]
    strip, half, sideways = HD // 4, HD // 8, 3
    tm = lax.axis_index("tm")
    tp = lax.axis_index("tp")
    lo, core = tp // 2, tp % 2
    x_hi, y, z = (tm // 8) % 2, tm // 16, tm % 8

    def shifted(by):
        return (lax.rem(tm + by + spans, spans), tp)

    peers = [(tm, lax.rem(tp + by, 4)) for by in (1, 2, 3)]
    across = [(tm + 8 - 16 * x_hi, (1 - lo) * 2 + c) for c in (0, 1)]
    sides = [[(tm, (1 - lo) * 2 + c) for c in (0, 1)], across]
    turn = jnp.where(z >= 4, 16, -16)
    y_next, y_prev = shifted(turn), shifted(-turn)
    turn_y = turn // 16

    def load(src, dst, slot, h):
        return pltpu.make_async_copy(
            src.at[:, pl.ds(pl.multiple_of(h * HD, HD), HD)], dst.at[h], load_sem.at[slot, h]
        )

    loads = [(q_hbm, q_own, 0), (k_hbm, k_own, 1), (v_hbm, v_own, 2)]
    for src, dst, slot in loads:
        for h in range(heads):
            load(src, dst, slot, h).start()

    first, last = z == 0, z == 7
    edge = jnp.logical_or(first, last)
    inner = jnp.logical_not(edge)
    opposite = [(y * 16 + (i // 4) * 8 + 7 - z, i % 4) for i in range(8)]
    barrier = pltpu.get_barrier_semaphore()
    greet = [shifted(1), shifted(-1), shifted(2), shifted(-2)] + peers + across + [y_prev]
    for other in greet:
        pl.semaphore_signal(barrier, inc=1, device_id=other, device_id_type=MESH)

    @pl.when(edge)
    def _():
        for other in opposite:
            pl.semaphore_signal(barrier, inc=1, device_id=other, device_id_type=MESH)

    w_own_copy = pltpu.make_async_copy(
        w_hbm.at[:, :, pl.ds(pl.multiple_of(tp * out_cols, HD), out_cols)],
        wbuf.at[:, tp],
        wload_sem,
    )
    w_own_copy.start()
    fresh_copy = pltpu.make_async_copy(fresh_hbm, fresh, fresh_sem)
    fresh_copy.start()

    def energy_of(ref):
        squares = jnp.zeros((rows, HD), F32)
        for h in range(heads):
            wide = ref[h].astype(F32)
            squares = squares + wide * wide
        return jnp.sum(jnp.transpose(squares), axis=0, keepdims=True)

    for src, dst, slot in loads[:2]:
        for h in range(heads):
            load(src, dst, slot, h).wait()
    energy_q = energy_of(q_own)
    energy_k = energy_of(k_own)
    line = lax.broadcasted_iota(jnp.int32, (8, rows), 0)
    message = jnp.where(line == 0, energy_q, 0.0)
    message = jnp.where(line == 1, energy_k, message)
    message = jnp.where(line == 2, reach_ref[0].astype(F32) * 0.25, message)
    message = jnp.where(line == 3, step_ref[0].astype(F32) * 0.25, message)
    est[tp] = message
    pl.semaphore_wait(barrier, len(greet) + len(opposite) * edge.astype(jnp.int32))

    def remote(src, dst, send, recv, to):
        return pltpu.make_async_remote_copy(
            src_ref=src, dst_ref=dst, send_sem=send, recv_sem=recv, device_id=to, device_id_type=MESH
        )

    up, down = shifted(1), shifted(-1)
    est_copies = [
        remote(est.at[tp], est.at[tp], est_s.at[i], est_r.at[tp], to) for i, to in enumerate(peers)
    ]

    def est_in(i):
        who = lax.rem(tp + i + 1, 4)
        return remote(est.at[who], est.at[who], est_s.at[i], est_r.at[who], peers[i])

    def q_copy(h):
        return remote(q_own.at[h], qa.at[h], q_s.at[h], q_r.at[h], up)

    def q_forward(h):
        return remote(qa.at[h], qb.at[h], qf_s.at[h], qf_r.at[h], up)

    def k_copy(h):
        return remote(k_own.at[h], k1.at[h], k_s.at[h], k_r.at[h], down)

    def v_copy(h):
        return remote(
            vt_own.at[h, pl.ds(0, HD), :], vt1.at[h, pl.ds(0, HD), :], v_s.at[h], v_r.at[h], down
        )

    def k_forward(h):
        return remote(k1.at[h], k2.at[h], kf_s.at[h], kf_r.at[h], down)

    def v_forward(h):
        return remote(
            vt1.at[h, pl.ds(0, HD), :], vt2.at[h, pl.ds(0, HD), :], vf_s.at[h], vf_r.at[h], down
        )

    def os_copy(h):
        return remote(os_out.at[h], os_in.at[h], os_s.at[h], os_r.at[h], up)

    def os_stat_copy(h):
        return remote(os_stat.at[h], os_in_stat.at[h], oss_s.at[h], oss_r.at[h], up)

    def far_copy(h):
        return remote(far_out.at[h], far_in.at[h], far_s.at[h], far_r.at[h], down)

    def far_stat_copy(h):
        return remote(far_stat.at[h], far_in_stat.at[h], fars_s.at[h], fars_r.at[h], down)

    parts = res_s.shape[0]
    part_rows = rows // parts

    def res_copy(i):
        cut = pl.ds(i * part_rows, part_rows)
        return remote(res_hbm.at[cut], res.at[cut], res_s.at[i], res_r.at[i], up)

    def st_copy(i, by):
        return remote(st_own, st_in.at[i], st_s.at[i], st_r.at[i], shifted(by))

    sibling = (tm, lo * 2 + 1 - core)

    def w_sibling():
        return remote(
            w_hbm.at[:, :, pl.ds(pl.multiple_of(sibling[1] * out_cols, HD), out_cols)],
            wbuf.at[:, tp],
            wsib_s,
            wsib_r,
            sibling,
        )

    def piece_rows(piece):
        return pl.ds(pl.multiple_of(piece * strip, strip), strip)

    def w_rows(side):
        return pl.ds(pl.multiple_of(y * strip + side * half, half), half)

    def w_import(side, c, part, some):
        to = sides[side][c]
        these = pl.ds(0, some)
        return remote(
            w_hbm.at[
                these, w_rows(part), pl.ds(pl.multiple_of(to[1] * out_cols, HD), out_cols)
            ],
            wbuf.at[these, tp, w_rows(part), :],
            wx_s.at[side, c],
            wx_r.at[side, core],
            to,
        )

    def w_import_in(side, c, part, some):
        slot = wbuf.at[pl.ds(0, some), (1 - lo) * 2 + c, w_rows(part), :]
        return remote(slot, slot, wx_s.at[side, c], wx_r.at[side, c], sides[side][c])

    def w_exports(act):
        @pl.when(inner)
        def _():
            for side in (0, 1):
                for c in (0, 1):
                    act(w_import(side, c, side, heads))

        for side in (0, 1):

            @pl.when(jnp.logical_and(edge, core == side))
            def _():
                for c in (0, 1):
                    act(w_import(side, c, 0, sideways))

    def w_piece(piece, h):
        return wbuf.at[h, pl.ds((1 - lo) * 2, 2), piece_rows(piece), :]

    def w_outward(h, to, rows_there):
        slot = wbuf.at[h, pl.ds((1 - lo) * 2, 2), rows_there, :]
        return remote(slot, slot, wz_s.at[h], wz_r.at[h], to)

    def outward(h, to, act):
        @pl.when(h < sideways)
        def _():
            act(w_outward(h, to, w_rows(1)))

        @pl.when(h >= sideways)
        def _():
            act(w_outward(h, to, piece_rows(y)))

    def w_along(k, h):
        slot = w_piece(lax.rem(y - turn_y * k + 4, 4), h)
        return remote(slot, slot, wy_s.at[k, h], wy_r.at[k, h], y_next)

    def w_along_in(k, h):
        slot = w_piece(lax.rem(y - turn_y * (k + 1) + 8, 4), h)
        return remote(slot, slot, wy_s.at[k, h], wy_r.at[k, h], y_next)

    half_rows = rows // 2

    def ag_slot(h, who, cut):
        return ag.at[h, who, cut]

    def unit(u):
        if isinstance(u, int) and u >= heads - 1:
            return heads - 1, pl.ds((u - heads + 1) * half_rows, half_rows)
        return u, pl.ds(0, rows)

    partner = (tm, (1 - lo) * 2 + core)
    diagonal = (1 - lo) * 2 + 1 - core

    def ag_move(i, u, who, to):
        h, cut = unit(u)
        slot = ag_slot(h, who, cut)
        return remote(slot, slot, ag_s.at[i, u], ag_r.at[who, u], to)

    def ag_copies(u):
        return [
            ag_move(0, u, tp, partner),
            ag_move(1, u, tp, sibling),
            ag_move(2, u, partner[1], sibling),
        ]

    def each(body):
        @pl.loop(0, heads)
        def _(h):
            body(h)

    def begin_up(some, end):
        @pl.loop(some, end)
        def _(h):
            q_copy(h).start()

    def begin_keys():
        for h in range(early):
            k_copy(h).start()

    def begin_values():
        for h in range(early):
            v_copy(h).start()

    def begin_rest():
        @pl.loop(early, heads)
        def _(h):
            k_copy(h).start()
            v_copy(h).start()

    early = 2
    for copy in est_copies:
        copy.start()
    pl.when(jnp.logical_not(first))(begin_keys)

    @pl.when(jnp.logical_not(last))
    def _():
        begin_up(0, early)

    w_exports(lambda copy: copy.start())

    ones = jnp.ones((16, rows), BF16)
    for h in range(heads):
        load(v_hbm, v_own, 2, h).wait()
        vt_own[h, :HD, :] = jnp.transpose(v_own[h])
        vt_own[h, HD : HD + 16, :] = ones
        if h == early - 1:
            pl.when(jnp.logical_not(first))(begin_values)

    for i in range(3):
        est_in(i).wait_recv()
    st_own[...] = est[0] + est[1] + est[2] + est[3]
    st_moves = [(0, 1), (1, 2), (2, -1), (3, -2)]
    for i, by in st_moves:
        st_copy(i, by).start()

    @pl.when(jnp.logical_not(last))
    def _():
        begin_up(early, heads)

    pl.when(jnp.logical_not(first))(begin_rest)
    for h in range(heads):
        both = q_gain_ref[h * HD : (h + 1) * HD] * k_gain_ref[h * HD : (h + 1) * HD]
        gain_buf[h] = both * (HD ** (-0.5) * LOG2E)
        vt1[h, HD : HD + 16, :] = ones
        vt2[h, HD : HD + 16, :] = ones

    def pass_weights():
        for side in (0, 1):
            for c in (0, 1):
                w_import_in(side, c, side, heads).wait_recv()

        @pl.loop(0, heads)
        def _(h):
            w_along(0, h).start()

            @pl.when(z == 1)
            def _():
                outward(h, down, lambda copy: copy.start())

            @pl.when(z == 6)
            def _():
                outward(h, up, lambda copy: copy.start())

    pl.when(inner)(pass_weights)

    @pl.when(edge)
    def _():
        for side in (0, 1):
            w_import_in(side, side, 0, sideways).wait_recv()
        for other in opposite:
            pl.semaphore_signal(gate_sem, inc=1, device_id=other, device_id_type=MESH)
        pl.semaphore_wait(gate_sem, len(opposite))

    @pl.when(last)
    def _():
        begin_up(0, heads)

    @pl.when(first)
    def _():
        begin_keys()
        begin_values()
        begin_rest()

    w_sibling().start()
    def begin_residual():
        for i in range(parts // 2):
            res_copy(i).start()

    pl.when(z != 6)(begin_residual)

    def column(state, row):
        scale = lax.rsqrt(state[row : row + 1, :] / width + EPS)
        return jnp.transpose(jnp.broadcast_to(scale, (HD, rows)))

    def unit_q(raw, scale, h):
        return (raw.astype(F32) * scale * gain_buf[pl.ds(h, 1), :]).astype(BF16)

    def unit_k(raw, scale):
        return (raw.astype(F32) * scale).astype(BF16)

    def scores_of(keys, queries):
        return lax.dot_general(
            keys, queries, (((1,), (1,)), ((), ())), preferred_element_type=F32
        )

    def alone(keys, queries, values):
        scores = scores_of(keys, queries)
        peak = jnp.max(scores, axis=0, keepdims=True)
        weight = jnp.exp2(scores - peak).astype(BF16)
        return jnp.dot(values, weight, preferred_element_type=F32), peak

    fold = rows // HD

    def pair(first, second):
        return jnp.concatenate(
            [one[:, i * HD : (i + 1) * HD] for one in (first, second) for i in range(fold)], axis=0
        )

    def unpair(packed):
        first = jnp.concatenate([packed[i : i + 1] for i in range(fold)], axis=1)
        second = jnp.concatenate([packed[fold + i : fold + i + 1] for i in range(fold)], axis=1)
        return first, second

    q_scale = column(st_own, 0)
    k_scale = column(st_own, 1)

    def self_part(h):
        q_copy(h).wait_recv()
        q_forward(h).start()
        kn[h] = unit_k(k_own[h], k_scale)
        mixed, peak = alone(kn[h], unit_q(q_own[h], q_scale, h), vt_own[h])
        os_out[h] = mixed[:HD].astype(BF16)
        os_stat[h] = pair(peak, mixed[HD : HD + 1])
        os_copy(h).start()
        os_stat_copy(h).start()

    each(self_part)
    pl.when(z == 6)(begin_residual)
    for i in range(parts // 2, parts):
        res_copy(i).start()

    st_copy(0, 1).wait_recv()
    state_a = st_in.at[0]
    reach = state_a[2:3, :]
    step = state_a[3:4, :1]
    place = lax.rem(pos_ref[0] + spans - 1, spans)

    def live(distance):
        inside = (place + distance <= spans - 1).astype(F32)
        return jnp.logical_and(reach >= distance, inside > 0.5)

    qa_scale = column(state_a, 0)

    def near_part(h):
        qn[h] = unit_q(qa[h], qa_scale, h)
        scores = scores_of(kn[h], qn[h])
        allowed = live(1)
        peak = jnp.max(scores, axis=0, keepdims=True)
        weight = jnp.exp2(scores - jnp.where(allowed, peak, MANY)).astype(BF16)
        acc[h] = jnp.dot(vt_own[h], weight, preferred_element_type=F32)
        top[h] = jnp.broadcast_to(jnp.where(allowed, peak, FEW), (8, rows))

    each(near_part)

    def join(h, keys, values, allowed):
        scores = scores_of(keys, qn[h])
        before = top[h][:1]
        peak = jnp.where(allowed, jnp.max(scores, axis=0, keepdims=True), FEW)
        after = jnp.maximum(before, peak)
        weight = jnp.exp2(scores - jnp.where(allowed, after, MANY)).astype(BF16)
        acc[h] = acc[h] * jnp.exp2(before - after) + jnp.dot(
            values, weight, preferred_element_type=F32
        )
        top[h] = jnp.broadcast_to(after, (8, rows))

    st_copy(2, -1).wait_recv()
    k1_scale = column(st_in.at[2], 1)

    def second_part(h):
        k_copy(h).wait_recv()
        k_forward(h).start()
        v_copy(h).wait_recv()
        v_forward(h).start()
        join(h, unit_k(k1[h], k1_scale), vt1[h], live(2))

        @pl.when(edge)
        def _():
            outward(h, up, lambda copy: copy.wait_recv())
            w_along(0, h).start()

    each(second_part)

    st_copy(1, 2).wait_recv()
    st_copy(3, -2).wait_recv()
    qb_scale = column(st_in.at[1], 0)
    k2_scale = column(st_in.at[3], 1)

    def third_part(h):
        q_forward(h).wait_recv()
        k_forward(h).wait_recv()
        v_forward(h).wait_recv()
        keys = unit_k(k2[h], k2_scale)
        mixed, peak = alone(keys, unit_q(qb[h], qb_scale, h), vt2[h])
        far_out[h] = mixed[:HD].astype(BF16)
        far_stat[h] = pair(peak, mixed[HD : HD + 1])
        far_copy(h).start()
        far_stat_copy(h).start()
        join(h, keys, vt2[h], live(3))
        w_along_in(0, h).wait_recv()
        w_along(1, h).start()

        @pl.when(h > 0)
        def _():
            w_along_in(1, h - 1).wait_recv()
            w_along(2, h - 1).start()

    each(third_part)
    w_along_in(1, heads - 1).wait_recv()
    w_along(2, heads - 1).start()

    def tiles(body):
        @pl.loop(0, out_cols // 256)
        def _(j):
            body(pl.ds(pl.multiple_of(j * 256, 256), 256))

    def product(h, cut):
        left = jnp.concatenate([ag[h, i] for i in range(4)], axis=1)
        return jnp.dot(left, wbuf[h, :, :, cut].reshape(4 * HD, 256), preferred_element_type=F32)

    def project(h):
        ag_move(0, h, sibling[1], sibling).wait_recv()
        ag_move(0, h, diagonal, sibling).wait_recv()
        w_along_in(2, h).wait_recv()

        def body(cut):
            total[:, cut] = total[:, cut] + product(h, cut)

        tiles(body)

    total[...] = jnp.zeros_like(total)

    def arrived(h):
        os_copy(h).wait_recv()
        os_stat_copy(h).wait_recv()
        far_copy(h).wait_recv()
        far_stat_copy(h).wait_recv()

    def merge(u):
        h, _ = unit(u)
        cut = slice(0, rows)
        if isinstance(u, int) and u >= heads - 1:
            cut = slice((u - heads + 1) * half_rows, (u - heads + 2) * half_rows)
        peak_s, sum_s = (one[:, cut] for one in unpair(os_in_stat[h]))
        peak_f, sum_f = (one[:, cut] for one in unpair(far_in_stat[h]))
        peak_m = top[h, :1, cut]
        peak_f = jnp.where(live(4)[:, cut], peak_f, FEW)
        peak = jnp.maximum(jnp.maximum(peak_s, peak_m), peak_f)
        by_s, by_m, by_f = jnp.exp2(peak_s - peak), jnp.exp2(peak_m - peak), jnp.exp2(peak_f - peak)
        mixed = acc[h, :, cut]
        whole = sum_s * by_s + mixed[HD : HD + 1] * by_m + sum_f * by_f
        share = 1.0 / whole
        attended = (
            os_in[h, :, cut].astype(F32) * (by_s * share)
            + mixed[:HD] * (by_m * share)
            + far_in[h, :, cut].astype(F32) * (by_f * share)
        )
        ag[h, tp, cut] = jnp.transpose(attended).astype(BF16)
        for copy in ag_copies(u)[:2]:
            copy.start()

    def relay(u):
        ag_move(0, u, partner[1], partner).wait_recv()
        ag_copies(u)[2].start()

    w_own_copy.wait()
    w_sibling().wait_recv()
    final = heads - 1
    for h in range(final):
        arrived(h)
        merge(h)
        if h >= 2:
            relay(h - 2)
        if h >= 3:
            project(h - 3)
    arrived(final)
    merge(final)
    merge(final + 1)
    for h in range(final - 2, final):
        relay(h)
        project(h - 1)
    for i in range(parts):
        res_copy(i).wait_recv()
    fresh_copy.wait()
    table = gate_ref[...].astype(F32)
    pick = lax.broadcasted_iota(jnp.int32, table.shape, 0).astype(F32) == step
    gate_buf[...] = jnp.sum(jnp.where(pick, table, 0.0), axis=0, keepdims=True)
    relay(final)
    relay(final + 1)
    project(final - 1)
    w_along_in(2, final).wait_recv()

    for u in (final, final + 1):
        ag_move(0, u, sibling[1], sibling).wait_recv()
        ag_move(0, u, diagonal, sibling).wait_recv()
        part = slice((u - final) * half_rows, (u - final + 1) * half_rows)

        def finish(cut, part=part):
            right = wbuf[final, :, :, cut].reshape(4 * HD, 256)
            left = jnp.concatenate([ag[final, i, part] for i in range(4)], axis=1)
            last_term = jnp.dot(left, right, preferred_element_type=F32)
            projected = total[part, cut] + last_term
            updated = (res[part, cut].astype(F32) + gate_buf[:, cut] * projected).astype(BF16)
            newest = jnp.full(updated.shape, pos_ref[0], jnp.int32) == 0
            out_ref[part, cut] = jnp.where(newest, fresh[part, cut], updated)

        tiles(finish)

    for copy in est_copies:
        copy.wait_send()
    for i, by in st_moves:
        st_copy(i, by).wait_send()
    for i in range(parts):
        res_copy(i).wait_send()
    w_sibling().wait_send()

    w_exports(lambda copy: copy.wait_send())

    @pl.when(jnp.logical_or(z == 1, z == 6))
    def _():
        @pl.loop(0, heads)
        def _(h):
            outward(h, down, lambda copy: copy.wait_send())

    def sent(h):
        for copy in (
            q_copy,
            q_forward,
            k_copy,
            v_copy,
            k_forward,
            v_forward,
            os_copy,
            os_stat_copy,
            far_copy,
            far_stat_copy,
        ):
            copy(h).wait_send()
        for i in range(3):
            w_along(i, h).wait_send()

    each(sent)
    for u in range(heads + 1):
        for copy in ag_copies(u):
            copy.wait_send()


def local(
    queries,
    key_rows,
    value_rows,
    query_gain,
    key_gain,
    out_weight,
    residual,
    gate_table,
    timesteps,
    windows,
    queue_positions,
    fresh_span,
):
    spans = lax.axis_size("tm")
    rows, width = queries.shape
    heads = width // HD
    out_cols = residual.shape[1]
    weight = out_weight.reshape(heads, HD, out_weight.shape[1])
    chunk = pltpu.VMEM((heads, rows, HD), BF16)
    flat = pltpu.VMEM((heads, HD, rows), BF16)
    tall = pltpu.VMEM((heads, HD + 16, rows), BF16)
    stats = pltpu.VMEM((heads, 8, rows), F32)
    packed = pltpu.VMEM((heads, 2 * (rows // HD), HD), F32)
    one = pltpu.SemaphoreType.DMA
    per_head = one((heads,))
    parts = 4
    hbm = pl.BlockSpec(memory_space=pl.ANY)
    vmem = pl.BlockSpec(memory_space=pltpu.VMEM)
    smem = pl.BlockSpec(memory_space=pltpu.SMEM)

    def run(*operands):
        def body(*refs):
            kernel(spans, *refs)

        return pl.pallas_call(
            body,
            out_shape=pltpu.VMEM((rows, out_cols), BF16),
            in_specs=[hbm, hbm, hbm, vmem, vmem, hbm, hbm, vmem, hbm, smem, smem, smem],
            out_specs=vmem,
            scratch_shapes=[
                chunk,
                chunk,
                chunk,
                tall,
                chunk,
                chunk,
                chunk,
                chunk,
                chunk,
                tall,
                chunk,
                tall,
                pltpu.VMEM((4, 8, rows), F32),
                pltpu.VMEM((8, rows), F32),
                pltpu.VMEM((4, 8, rows), F32),
                flat,
                packed,
                flat,
                packed,
                flat,
                packed,
                flat,
                packed,
                pltpu.VMEM((heads, HD + 16, rows), F32),
                stats,
                pltpu.VMEM((heads, 4, rows, HD), BF16),
                pltpu.VMEM((heads, 4, HD, out_cols), BF16),
                pltpu.VMEM((rows, out_cols), BF16),
                pltpu.VMEM((rows, out_cols), F32),
                pltpu.VMEM((heads, HD), F32),
                pltpu.VMEM((1, out_cols), F32),
                pltpu.VMEM((rows, out_cols), BF16),
                one((3, heads)),
                one,
                one,
                one((3,)),
                one((4,)),
                one((4,)),
                one((4,)),
                per_head,
                per_head,
                per_head,
                per_head,
                per_head,
                per_head,
                per_head,
                per_head,
                per_head,
                per_head,
                per_head,
                per_head,
                per_head,
                per_head,
                per_head,
                per_head,
                per_head,
                per_head,
                per_head,
                per_head,
                one((parts,)),
                one((parts,)),
                one,
                one,
                one((2, 2)),
                one((2, 2)),
                one((3, heads)),
                one((3, heads)),
                one((3, heads + 1)),
                one((4, heads + 1)),
                per_head,
                per_head,
                pltpu.SemaphoreType.REGULAR,
            ],
            compiler_params=pltpu.CompilerParams(
                collective_id=0, has_side_effects=True, vmem_limit_bytes=56 * 2**20
            ),
            name="window_block",
        )(*operands)

    return run(
        queries,
        key_rows,
        value_rows,
        query_gain,
        key_gain,
        weight,
        residual,
        gate_table,
        fresh_span,
        timesteps,
        windows,
        queue_positions,
    )


def solution(mesh):
    placed = (
        P("tm", "tp"),
        P("tm", "tp"),
        P("tm", "tp"),
        P("tp"),
        P("tp"),
        P("tp", None),
        P("tm", "tp"),
        P(None, "tp"),
        P("tm"),
        P("tm"),
        P("tm"),
        P(None, "tp"),
    )
    return jax.shard_map(
        local, mesh=mesh, in_specs=placed, out_specs=P("tm", "tp"), check_vma=False
    )
```

```python
import jax
import jax.numpy as jnp
from jax import lax
from jax.experimental import pallas as pl
from jax.experimental.pallas import tpu as pltpu
from jax.sharding import PartitionSpec as P

HD = 128
WMAX = 4
EPS = 1e-06
FEW = -1e30
MANY = 1e30
LOG2E = 1.4426950408889634
MESH = pl.DeviceIdType.MESH
F32 = jnp.float32
BF16 = jnp.bfloat16


def kernel(
    spans,
    q_hbm,
    k_hbm,
    v_hbm,
    q_gain_ref,
    k_gain_ref,
    w_hbm,
    res_hbm,
    gate_ref,
    fresh_hbm,
    step_ref,
    reach_ref,
    pos_ref,
    out_ref,
    q_own,
    k_own,
    v_own,
    vt_own,
    qn,
    kn,
    qa,
    qb,
    k1,
    vt1,
    k2,
    vt2,
    est,
    st_own,
    st_in,
    os_out,
    os_stat,
    os_in,
    os_in_stat,
    far_out,
    far_stat,
    far_in,
    far_in_stat,
    acc,
    top,
    ag,
    wbuf,
    res,
    total,
    gain_buf,
    gate_buf,
    fresh,
    load_sem,
    wload_sem,
    fresh_sem,
    est_s,
    est_r,
    st_s,
    st_r,
    q_s,
    q_r,
    qf_s,
    qf_r,
    k_s,
    k_r,
    v_s,
    v_r,
    kf_s,
    kf_r,
    vf_s,
    vf_r,
    os_s,
    os_r,
    oss_s,
    oss_r,
    far_s,
    far_r,
    fars_s,
    fars_r,
    res_s,
    res_r,
    wsib_s,
    wsib_r,
    wx_s,
    wx_r,
    wy_s,
    wy_r,
    ag_s,
    ag_r,
    wz_s,
    wz_r,
    gate_sem,
):
    heads, rows = q_own.shape[0], q_own.shape[1]
    local = heads * HD
    width = 4 * local
    out_cols = out_ref.shape[1]
    strip, half, sideways = HD // 4, HD // 8, 3
    tm = lax.axis_index("tm")
    tp = lax.axis_index("tp")
    lo, core = tp // 2, tp % 2
    x_hi, y, z = (tm // 8) % 2, tm // 16, tm % 8

    def shifted(by):
        return (lax.rem(tm + by + spans, spans), tp)

    peers = [(tm, lax.rem(tp + by, 4)) for by in (1, 2, 3)]
    across = [(tm + 8 - 16 * x_hi, (1 - lo) * 2 + c) for c in (0, 1)]
    sides = [[(tm, (1 - lo) * 2 + c) for c in (0, 1)], across]
    turn = jnp.where(z >= 4, 16, -16)
    y_next, y_prev = shifted(turn), shifted(-turn)
    turn_y = turn // 16

    def load(src, dst, slot, h):
        return pltpu.make_async_copy(
            src.at[:, pl.ds(pl.multiple_of(h * HD, HD), HD)], dst.at[h], load_sem.at[slot, h]
        )

    loads = [(q_hbm, q_own, 0), (k_hbm, k_own, 1), (v_hbm, v_own, 2)]
    for src, dst, slot in loads:
        for h in range(heads):
            load(src, dst, slot, h).start()

    first, last = z == 0, z == 7
    edge = jnp.logical_or(first, last)
    inner = jnp.logical_not(edge)
    opposite = [(y * 16 + (i // 4) * 8 + 7 - z, i % 4) for i in range(8)]
    barrier = pltpu.get_barrier_semaphore()
    greet = [shifted(1), shifted(-1), shifted(2), shifted(-2)] + peers + across + [y_prev]
    for other in greet:
        pl.semaphore_signal(barrier, inc=1, device_id=other, device_id_type=MESH)

    @pl.when(edge)
    def _():
        for other in opposite:
            pl.semaphore_signal(barrier, inc=1, device_id=other, device_id_type=MESH)

    w_own_copy = pltpu.make_async_copy(
        w_hbm.at[:, :, pl.ds(pl.multiple_of(tp * out_cols, HD), out_cols)],
        wbuf.at[:, tp],
        wload_sem,
    )
    w_own_copy.start()
    fresh_copy = pltpu.make_async_copy(fresh_hbm, fresh, fresh_sem)
    fresh_copy.start()

    def energy_of(ref):
        squares = jnp.zeros((rows, HD), F32)
        for h in range(heads):
            wide = ref[h].astype(F32)
            squares = squares + wide * wide
        return jnp.sum(jnp.transpose(squares), axis=0, keepdims=True)

    for src, dst, slot in loads[:2]:
        for h in range(heads):
            load(src, dst, slot, h).wait()
    energy_q = energy_of(q_own)
    energy_k = energy_of(k_own)
    line = lax.broadcasted_iota(jnp.int32, (8, rows), 0)
    message = jnp.where(line == 0, energy_q, 0.0)
    message = jnp.where(line == 1, energy_k, message)
    message = jnp.where(line == 2, reach_ref[0].astype(F32) * 0.25, message)
    message = jnp.where(line == 3, step_ref[0].astype(F32) * 0.25, message)
    est[tp] = message
    pl.semaphore_wait(barrier, len(greet) + len(opposite) * edge.astype(jnp.int32))

    def remote(src, dst, send, recv, to):
        return pltpu.make_async_remote_copy(
            src_ref=src, dst_ref=dst, send_sem=send, recv_sem=recv, device_id=to, device_id_type=MESH
        )

    up, down = shifted(1), shifted(-1)
    est_copies = [
        remote(est.at[tp], est.at[tp], est_s.at[i], est_r.at[tp], to) for i, to in enumerate(peers)
    ]

    def est_in(i):
        who = lax.rem(tp + i + 1, 4)
        return remote(est.at[who], est.at[who], est_s.at[i], est_r.at[who], peers[i])

    def q_copy(h):
        return remote(q_own.at[h], qa.at[h], q_s.at[h], q_r.at[h], up)

    def q_forward(h):
        return remote(qa.at[h], qb.at[h], qf_s.at[h], qf_r.at[h], up)

    def k_copy(h):
        return remote(k_own.at[h], k1.at[h], k_s.at[h], k_r.at[h], down)

    def v_copy(h):
        return remote(
            vt_own.at[h, pl.ds(0, HD), :], vt1.at[h, pl.ds(0, HD), :], v_s.at[h], v_r.at[h], down
        )

    def k_forward(h):
        return remote(k1.at[h], k2.at[h], kf_s.at[h], kf_r.at[h], down)

    def v_forward(h):
        return remote(
            vt1.at[h, pl.ds(0, HD), :], vt2.at[h, pl.ds(0, HD), :], vf_s.at[h], vf_r.at[h], down
        )

    def os_copy(h):
        return remote(os_out.at[h], os_in.at[h], os_s.at[h], os_r.at[h], up)

    def os_stat_copy(h):
        return remote(os_stat.at[h], os_in_stat.at[h], oss_s.at[h], oss_r.at[h], up)

    def far_copy(h):
        return remote(far_out.at[h], far_in.at[h], far_s.at[h], far_r.at[h], down)

    def far_stat_copy(h):
        return remote(far_stat.at[h], far_in_stat.at[h], fars_s.at[h], fars_r.at[h], down)

    parts = res_s.shape[0]
    part_rows = rows // parts

    def res_copy(i):
        cut = pl.ds(i * part_rows, part_rows)
        return remote(res_hbm.at[cut], res.at[cut], res_s.at[i], res_r.at[i], up)

    def st_copy(i, by):
        return remote(st_own, st_in.at[i], st_s.at[i], st_r.at[i], shifted(by))

    sibling = (tm, lo * 2 + 1 - core)

    def w_sibling():
        return remote(
            w_hbm.at[:, :, pl.ds(pl.multiple_of(sibling[1] * out_cols, HD), out_cols)],
            wbuf.at[:, tp],
            wsib_s,
            wsib_r,
            sibling,
        )

    def piece_rows(piece):
        return pl.ds(pl.multiple_of(piece * strip, strip), strip)

    def w_rows(side):
        return pl.ds(pl.multiple_of(y * strip + side * half, half), half)

    def w_import(side, c, part, some):
        to = sides[side][c]
        these = pl.ds(0, some)
        return remote(
            w_hbm.at[
                these, w_rows(part), pl.ds(pl.multiple_of(to[1] * out_cols, HD), out_cols)
            ],
            wbuf.at[these, tp, w_rows(part), :],
            wx_s.at[side, c],
            wx_r.at[side, core],
            to,
        )

    def w_import_in(side, c, part, some):
        slot = wbuf.at[pl.ds(0, some), (1 - lo) * 2 + c, w_rows(part), :]
        return remote(slot, slot, wx_s.at[side, c], wx_r.at[side, c], sides[side][c])

    def w_exports(act):
        @pl.when(inner)
        def _():
            for side in (0, 1):
                for c in (0, 1):
                    act(w_import(side, c, side, heads))

        for side in (0, 1):

            @pl.when(jnp.logical_and(edge, core == side))
            def _():
                for c in (0, 1):
                    act(w_import(side, c, 0, sideways))

    def w_piece(piece, h):
        return wbuf.at[h, pl.ds((1 - lo) * 2, 2), piece_rows(piece), :]

    def w_outward(h, to, rows_there):
        slot = wbuf.at[h, pl.ds((1 - lo) * 2, 2), rows_there, :]
        return remote(slot, slot, wz_s.at[h], wz_r.at[h], to)

    def outward(h, to, act):
        @pl.when(h < sideways)
        def _():
            act(w_outward(h, to, w_rows(1)))

        @pl.when(h >= sideways)
        def _():
            act(w_outward(h, to, piece_rows(y)))

    def w_along(k, h):
        slot = w_piece(lax.rem(y - turn_y * k + 4, 4), h)
        return remote(slot, slot, wy_s.at[k, h], wy_r.at[k, h], y_next)

    def w_along_in(k, h):
        slot = w_piece(lax.rem(y - turn_y * (k + 1) + 8, 4), h)
        return remote(slot, slot, wy_s.at[k, h], wy_r.at[k, h], y_next)

    half_rows = rows // 2

    def ag_slot(h, who, cut):
        return ag.at[h, who, cut]

    def unit(u):
        if isinstance(u, int) and u >= heads - 1:
            return heads - 1, pl.ds((u - heads + 1) * half_rows, half_rows)
        return u, pl.ds(0, rows)

    partner = (tm, (1 - lo) * 2 + core)
    diagonal = (1 - lo) * 2 + 1 - core

    def ag_move(i, u, who, to):
        h, cut = unit(u)
        slot = ag_slot(h, who, cut)
        return remote(slot, slot, ag_s.at[i, u], ag_r.at[who, u], to)

    def ag_copies(u):
        return [
            ag_move(0, u, tp, partner),
            ag_move(1, u, tp, sibling),
            ag_move(2, u, partner[1], sibling),
        ]

    def each(body):
        @pl.loop(0, heads)
        def _(h):
            body(h)

    def begin_up(some, end):
        @pl.loop(some, end)
        def _(h):
            q_copy(h).start()

    def begin_keys():
        for h in range(early):
            k_copy(h).start()

    def begin_values():
        for h in range(early):
            v_copy(h).start()

    def begin_rest():
        @pl.loop(early, heads)
        def _(h):
            k_copy(h).start()
            v_copy(h).start()

    early = 2
    for copy in est_copies:
        copy.start()
    pl.when(jnp.logical_not(first))(begin_keys)

    @pl.when(jnp.logical_not(last))
    def _():
        begin_up(0, early)

    w_exports(lambda copy: copy.start())

    ones = jnp.ones((16, rows), BF16)
    for h in range(heads):
        load(v_hbm, v_own, 2, h).wait()
        vt_own[h, :HD, :] = jnp.transpose(v_own[h])
        vt_own[h, HD : HD + 16, :] = ones
        if h == early - 1:
            pl.when(jnp.logical_not(first))(begin_values)

    for i in range(3):
        est_in(i).wait_recv()
    st_own[...] = est[0] + est[1] + est[2] + est[3]
    st_moves = [(0, 1), (1, 2), (2, -1), (3, -2)]
    for i, by in st_moves:
        st_copy(i, by).start()

    @pl.when(jnp.logical_not(last))
    def _():
        begin_up(early, heads)

    pl.when(jnp.logical_not(first))(begin_rest)
    for h in range(heads):
        both = q_gain_ref[h * HD : (h + 1) * HD] * k_gain_ref[h * HD : (h + 1) * HD]
        gain_buf[h] = both * (HD ** (-0.5) * LOG2E)
        vt1[h, HD : HD + 16, :] = ones
        vt2[h, HD : HD + 16, :] = ones

    def pass_weights():
        for side in (0, 1):
            for c in (0, 1):
                w_import_in(side, c, side, heads).wait_recv()

        @pl.loop(0, heads)
        def _(h):
            w_along(0, h).start()

            @pl.when(z == 1)
            def _():
                outward(h, down, lambda copy: copy.start())

            @pl.when(z == 6)
            def _():
                outward(h, up, lambda copy: copy.start())

    pl.when(inner)(pass_weights)

    @pl.when(edge)
    def _():
        for side in (0, 1):
            w_import_in(side, side, 0, sideways).wait_recv()
        for other in opposite:
            pl.semaphore_signal(gate_sem, inc=1, device_id=other, device_id_type=MESH)
        pl.semaphore_wait(gate_sem, len(opposite))

    @pl.when(last)
    def _():
        begin_up(0, heads)

    @pl.when(first)
    def _():
        begin_keys()
        begin_values()
        begin_rest()

    w_sibling().start()
    def begin_residual():
        for i in range(parts // 2):
            res_copy(i).start()

    pl.when(z != 6)(begin_residual)

    def column(state, row):
        scale = lax.rsqrt(state[row : row + 1, :] / width + EPS)
        return jnp.transpose(jnp.broadcast_to(scale, (HD, rows)))

    def unit_q(raw, scale, h):
        return (raw.astype(F32) * scale * gain_buf[pl.ds(h, 1), :]).astype(BF16)

    def unit_k(raw, scale):
        return (raw.astype(F32) * scale).astype(BF16)

    def scores_of(keys, queries):
        return lax.dot_general(
            keys, queries, (((1,), (1,)), ((), ())), preferred_element_type=F32
        )

    def alone(keys, queries, values):
        scores = scores_of(keys, queries)
        peak = jnp.max(scores, axis=0, keepdims=True)
        weight = jnp.exp2(scores - peak).astype(BF16)
        return jnp.dot(values, weight, preferred_element_type=F32), peak

    fold = rows // HD

    def pair(first, second):
        return jnp.concatenate(
            [one[:, i * HD : (i + 1) * HD] for one in (first, second) for i in range(fold)], axis=0
        )

    def unpair(packed):
        first = jnp.concatenate([packed[i : i + 1] for i in range(fold)], axis=1)
        second = jnp.concatenate([packed[fold + i : fold + i + 1] for i in range(fold)], axis=1)
        return first, second

    q_scale = column(st_own, 0)
    k_scale = column(st_own, 1)

    def self_part(h):
        q_copy(h).wait_recv()
        q_forward(h).start()
        kn[h] = unit_k(k_own[h], k_scale)
        mixed, peak = alone(kn[h], unit_q(q_own[h], q_scale, h), vt_own[h])
        os_out[h] = mixed[:HD].astype(BF16)
        os_stat[h] = pair(peak, mixed[HD : HD + 1])
        os_copy(h).start()
        os_stat_copy(h).start()

    each(self_part)
    pl.when(z == 6)(begin_residual)
    for i in range(parts // 2, parts):
        res_copy(i).start()

    st_copy(0, 1).wait_recv()
    state_a = st_in.at[0]
    reach = state_a[2:3, :]
    step = state_a[3:4, :1]
    place = lax.rem(pos_ref[0] + spans - 1, spans)

    def live(distance):
        inside = (place + distance <= spans - 1).astype(F32)
        return jnp.logical_and(reach >= distance, inside > 0.5)

    qa_scale = column(state_a, 0)

    def near_part(h):
        qn[h] = unit_q(qa[h], qa_scale, h)
        scores = scores_of(kn[h], qn[h])
        allowed = live(1)
        peak = jnp.max(scores, axis=0, keepdims=True)
        weight = jnp.exp2(scores - jnp.where(allowed, peak, MANY)).astype(BF16)
        acc[h] = jnp.dot(vt_own[h], weight, preferred_element_type=F32)
        top[h] = jnp.broadcast_to(jnp.where(allowed, peak, FEW), (8, rows))

    each(near_part)

    def join(h, keys, values, allowed):
        scores = scores_of(keys, qn[h])
        before = top[h][:1]
        peak = jnp.where(allowed, jnp.max(scores, axis=0, keepdims=True), FEW)
        after = jnp.maximum(before, peak)
        weight = jnp.exp2(scores - jnp.where(allowed, after, MANY)).astype(BF16)
        acc[h] = acc[h] * jnp.exp2(before - after) + jnp.dot(
            values, weight, preferred_element_type=F32
        )
        top[h] = jnp.broadcast_to(after, (8, rows))

    st_copy(2, -1).wait_recv()
    k1_scale = column(st_in.at[2], 1)

    def second_part(h):
        k_copy(h).wait_recv()
        k_forward(h).start()
        v_copy(h).wait_recv()
        v_forward(h).start()
        join(h, unit_k(k1[h], k1_scale), vt1[h], live(2))

        @pl.when(edge)
        def _():
            outward(h, up, lambda copy: copy.wait_recv())
            w_along(0, h).start()

    each(second_part)

    st_copy(1, 2).wait_recv()
    st_copy(3, -2).wait_recv()
    qb_scale = column(st_in.at[1], 0)
    k2_scale = column(st_in.at[3], 1)

    def third_part(h):
        q_forward(h).wait_recv()
        k_forward(h).wait_recv()
        v_forward(h).wait_recv()
        keys = unit_k(k2[h], k2_scale)
        mixed, peak = alone(keys, unit_q(qb[h], qb_scale, h), vt2[h])
        far_out[h] = mixed[:HD].astype(BF16)
        far_stat[h] = pair(peak, mixed[HD : HD + 1])
        far_copy(h).start()
        far_stat_copy(h).start()
        join(h, keys, vt2[h], live(3))
        w_along_in(0, h).wait_recv()
        w_along(1, h).start()

        @pl.when(h > 0)
        def _():
            w_along_in(1, h - 1).wait_recv()
            w_along(2, h - 1).start()

    each(third_part)
    w_along_in(1, heads - 1).wait_recv()
    w_along(2, heads - 1).start()

    def tiles(body):
        @pl.loop(0, out_cols // 256)
        def _(j):
            body(pl.ds(pl.multiple_of(j * 256, 256), 256))

    def product(h, cut):
        left = jnp.concatenate([ag[h, i] for i in range(4)], axis=1)
        return jnp.dot(left, wbuf[h, :, :, cut].reshape(4 * HD, 256), preferred_element_type=F32)

    def project(h):
        ag_move(0, h, sibling[1], sibling).wait_recv()
        ag_move(0, h, diagonal, sibling).wait_recv()
        w_along_in(2, h).wait_recv()

        def body(cut):
            total[:, cut] = total[:, cut] + product(h, cut)

        tiles(body)

    total[...] = jnp.zeros_like(total)

    def arrived(h):
        os_copy(h).wait_recv()
        os_stat_copy(h).wait_recv()
        far_copy(h).wait_recv()
        far_stat_copy(h).wait_recv()

    def merge(u):
        h, _ = unit(u)
        cut = slice(0, rows)
        if isinstance(u, int) and u >= heads - 1:
            cut = slice((u - heads + 1) * half_rows, (u - heads + 2) * half_rows)
        peak_s, sum_s = (one[:, cut] for one in unpair(os_in_stat[h]))
        peak_f, sum_f = (one[:, cut] for one in unpair(far_in_stat[h]))
        peak_m = top[h, :1, cut]
        peak_f = jnp.where(live(4)[:, cut], peak_f, FEW)
        peak = jnp.maximum(jnp.maximum(peak_s, peak_m), peak_f)
        by_s, by_m, by_f = jnp.exp2(peak_s - peak), jnp.exp2(peak_m - peak), jnp.exp2(peak_f - peak)
        mixed = acc[h, :, cut]
        whole = sum_s * by_s + mixed[HD : HD + 1] * by_m + sum_f * by_f
        share = 1.0 / whole
        attended = (
            os_in[h, :, cut].astype(F32) * (by_s * share)
            + mixed[:HD] * (by_m * share)
            + far_in[h, :, cut].astype(F32) * (by_f * share)
        )
        ag[h, tp, cut] = jnp.transpose(attended).astype(BF16)
        for copy in ag_copies(u)[:2]:
            copy.start()

    def relay(u):
        ag_move(0, u, partner[1], partner).wait_recv()
        ag_copies(u)[2].start()

    w_own_copy.wait()
    w_sibling().wait_recv()
    final = heads - 1
    for h in range(final):
        arrived(h)
        merge(h)
        if h >= 2:
            relay(h - 2)
        if h >= 3:
            project(h - 3)
    arrived(final)
    merge(final)
    merge(final + 1)
    for h in range(final - 2, final):
        relay(h)
        project(h - 1)
    for i in range(parts):
        res_copy(i).wait_recv()
    fresh_copy.wait()
    table = gate_ref[...].astype(F32)
    pick = lax.broadcasted_iota(jnp.int32, table.shape, 0).astype(F32) == step
    gate_buf[...] = jnp.sum(jnp.where(pick, table, 0.0), axis=0, keepdims=True)
    for copy in est_copies:
        copy.wait_send()
    for i, by in st_moves:
        st_copy(i, by).wait_send()
    for i in range(parts):
        res_copy(i).wait_send()
    w_sibling().wait_send()

    w_exports(lambda copy: copy.wait_send())

    @pl.when(jnp.logical_or(z == 1, z == 6))
    def _():
        @pl.loop(0, heads)
        def _(h):
            outward(h, down, lambda copy: copy.wait_send())

    def sent(h):
        for copy in (
            q_copy,
            q_forward,
            k_copy,
            v_copy,
            k_forward,
            v_forward,
            os_copy,
            os_stat_copy,
            far_copy,
            far_stat_copy,
        ):
            copy(h).wait_send()
        for i in range(3):
            w_along(i, h).wait_send()

    each(sent)

    relay(final)
    relay(final + 1)
    project(final - 1)
    w_along_in(2, final).wait_recv()

    for u in (final, final + 1):
        ag_move(0, u, sibling[1], sibling).wait_recv()
        ag_move(0, u, diagonal, sibling).wait_recv()
        part = slice((u - final) * half_rows, (u - final + 1) * half_rows)

        def finish(cut, part=part):
            right = wbuf[final, :, :, cut].reshape(4 * HD, 256)
            left = jnp.concatenate([ag[final, i, part] for i in range(4)], axis=1)
            last_term = jnp.dot(left, right, preferred_element_type=F32)
            projected = total[part, cut] + last_term
            updated = (res[part, cut].astype(F32) + gate_buf[:, cut] * projected).astype(BF16)
            newest = jnp.full(updated.shape, pos_ref[0], jnp.int32) == 0
            out_ref[part, cut] = jnp.where(newest, fresh[part, cut], updated)

        tiles(finish)

    for u in range(heads + 1):
        for copy in ag_copies(u):
            copy.wait_send()


def local(
    queries,
    key_rows,
    value_rows,
    query_gain,
    key_gain,
    out_weight,
    residual,
    gate_table,
    timesteps,
    windows,
    queue_positions,
    fresh_span,
):
    spans = lax.axis_size("tm")
    rows, width = queries.shape
    heads = width // HD
    out_cols = residual.shape[1]
    weight = out_weight.reshape(heads, HD, out_weight.shape[1])
    chunk = pltpu.VMEM((heads, rows, HD), BF16)
    flat = pltpu.VMEM((heads, HD, rows), BF16)
    tall = pltpu.VMEM((heads, HD + 16, rows), BF16)
    stats = pltpu.VMEM((heads, 8, rows), F32)
    packed = pltpu.VMEM((heads, 2 * (rows // HD), HD), F32)
    one = pltpu.SemaphoreType.DMA
    per_head = one((heads,))
    parts = 4
    hbm = pl.BlockSpec(memory_space=pl.ANY)
    vmem = pl.BlockSpec(memory_space=pltpu.VMEM)
    smem = pl.BlockSpec(memory_space=pltpu.SMEM)

    def run(*operands):
        def body(*refs):
            kernel(spans, *refs)

        return pl.pallas_call(
            body,
            out_shape=pltpu.VMEM((rows, out_cols), BF16),
            in_specs=[hbm, hbm, hbm, vmem, vmem, hbm, hbm, vmem, hbm, smem, smem, smem],
            out_specs=vmem,
            scratch_shapes=[
                chunk,
                chunk,
                chunk,
                tall,
                chunk,
                chunk,
                chunk,
                chunk,
                chunk,
                tall,
                chunk,
                tall,
                pltpu.VMEM((4, 8, rows), F32),
                pltpu.VMEM((8, rows), F32),
                pltpu.VMEM((4, 8, rows), F32),
                flat,
                packed,
                flat,
                packed,
                flat,
                packed,
                flat,
                packed,
                pltpu.VMEM((heads, HD + 16, rows), F32),
                stats,
                pltpu.VMEM((heads, 4, rows, HD), BF16),
                pltpu.VMEM((heads, 4, HD, out_cols), BF16),
                pltpu.VMEM((rows, out_cols), BF16),
                pltpu.VMEM((rows, out_cols), F32),
                pltpu.VMEM((heads, HD), F32),
                pltpu.VMEM((1, out_cols), F32),
                pltpu.VMEM((rows, out_cols), BF16),
                one((3, heads)),
                one,
                one,
                one((3,)),
                one((4,)),
                one((4,)),
                one((4,)),
                per_head,
                per_head,
                per_head,
                per_head,
                per_head,
                per_head,
                per_head,
                per_head,
                per_head,
                per_head,
                per_head,
                per_head,
                per_head,
                per_head,
                per_head,
                per_head,
                per_head,
                per_head,
                per_head,
                per_head,
                one((parts,)),
                one((parts,)),
                one,
                one,
                one((2, 2)),
                one((2, 2)),
                one((3, heads)),
                one((3, heads)),
                one((3, heads + 1)),
                one((4, heads + 1)),
                per_head,
                per_head,
                pltpu.SemaphoreType.REGULAR,
            ],
            compiler_params=pltpu.CompilerParams(
                collective_id=0, has_side_effects=True, vmem_limit_bytes=56 * 2**20
            ),
            name="window_block",
        )(*operands)

    return run(
        queries,
        key_rows,
        value_rows,
        query_gain,
        key_gain,
        weight,
        residual,
        gate_table,
        fresh_span,
        timesteps,
        windows,
        queue_positions,
    )


def solution(mesh):
    placed = (
        P("tm", "tp"),
        P("tm", "tp"),
        P("tm", "tp"),
        P("tp"),
        P("tp"),
        P("tp", None),
        P("tm", "tp"),
        P(None, "tp"),
        P("tm"),
        P("tm"),
        P("tm"),
        P(None, "tp"),
    )
    return jax.shard_map(
        local, mesh=mesh, in_specs=placed, out_specs=P("tm", "tp"), check_vma=False
    )
```

```python
import jax
import jax.numpy as jnp
from jax import lax
from jax.experimental import pallas as pl
from jax.experimental.pallas import tpu as pltpu
from jax.sharding import PartitionSpec as P

HD = 128
WMAX = 4
EPS = 1e-06
FEW = -1e30
MANY = 1e30
LOG2E = 1.4426950408889634
MESH = pl.DeviceIdType.MESH
F32 = jnp.float32
BF16 = jnp.bfloat16


def kernel(
    spans,
    q_hbm,
    k_hbm,
    v_hbm,
    q_gain_ref,
    k_gain_ref,
    w_hbm,
    res_hbm,
    gate_ref,
    fresh_hbm,
    step_ref,
    reach_ref,
    pos_ref,
    out_ref,
    q_own,
    k_own,
    v_own,
    vt_own,
    qn,
    kn,
    qa,
    qb,
    k1,
    vt1,
    k2,
    vt2,
    est,
    st_own,
    st_in,
    os_out,
    os_stat,
    os_in,
    os_in_stat,
    far_out,
    far_stat,
    far_in,
    far_in_stat,
    acc,
    top,
    ag,
    wbuf,
    res,
    total,
    gain_buf,
    gate_buf,
    fresh,
    load_sem,
    wload_sem,
    fresh_sem,
    est_s,
    est_r,
    st_s,
    st_r,
    q_s,
    q_r,
    qf_s,
    qf_r,
    k_s,
    k_r,
    v_s,
    v_r,
    kf_s,
    kf_r,
    vf_s,
    vf_r,
    os_s,
    os_r,
    oss_s,
    oss_r,
    far_s,
    far_r,
    fars_s,
    fars_r,
    res_s,
    res_r,
    wsib_s,
    wsib_r,
    wx_s,
    wx_r,
    wy_s,
    wy_r,
    ag_s,
    ag_r,
    wz_s,
    wz_r,
    gate_sem,
):
    heads, rows = q_own.shape[0], q_own.shape[1]
    local = heads * HD
    width = 4 * local
    out_cols = out_ref.shape[1]
    strip, half, sideways = HD // 4, HD // 8, 3
    tm = lax.axis_index("tm")
    tp = lax.axis_index("tp")
    lo, core = tp // 2, tp % 2
    x_hi, y, z = (tm // 8) % 2, tm // 16, tm % 8

    def shifted(by):
        return (lax.rem(tm + by + spans, spans), tp)

    peers = [(tm, lax.rem(tp + by, 4)) for by in (1, 2, 3)]
    across = [(tm + 8 - 16 * x_hi, (1 - lo) * 2 + c) for c in (0, 1)]
    sides = [[(tm, (1 - lo) * 2 + c) for c in (0, 1)], across]
    turn = jnp.where(z >= 4, 16, -16)
    y_next, y_prev = shifted(turn), shifted(-turn)
    turn_y = turn // 16

    def load(src, dst, slot, h):
        return pltpu.make_async_copy(
            src.at[:, pl.ds(pl.multiple_of(h * HD, HD), HD)], dst.at[h], load_sem.at[slot, h]
        )

    loads = [(q_hbm, q_own, 0), (k_hbm, k_own, 1), (v_hbm, v_own, 2)]
    for src, dst, slot in loads:
        for h in range(heads):
            load(src, dst, slot, h).start()

    first, last = z == 0, z == 7
    edge = jnp.logical_or(first, last)
    inner = jnp.logical_not(edge)
    opposite = [(y * 16 + (i // 4) * 8 + 7 - z, i % 4) for i in range(8)]
    barrier = pltpu.get_barrier_semaphore()
    greet = [shifted(1), shifted(-1), shifted(2), shifted(-2)] + peers + across + [y_prev]
    for other in greet:
        pl.semaphore_signal(barrier, inc=1, device_id=other, device_id_type=MESH)

    @pl.when(edge)
    def _():
        for other in opposite:
            pl.semaphore_signal(barrier, inc=1, device_id=other, device_id_type=MESH)

    w_own_copy = pltpu.make_async_copy(
        w_hbm.at[:, :, pl.ds(pl.multiple_of(tp * out_cols, HD), out_cols)],
        wbuf.at[:, tp],
        wload_sem,
    )
    w_own_copy.start()
    fresh_copy = pltpu.make_async_copy(fresh_hbm, fresh, fresh_sem)
    fresh_copy.start()

    def energy_of(ref):
        squares = jnp.zeros((rows, HD), F32)
        for h in range(heads):
            wide = ref[h].astype(F32)
            squares = squares + wide * wide
        return jnp.sum(jnp.transpose(squares), axis=0, keepdims=True)

    for src, dst, slot in loads[:2]:
        for h in range(heads):
            load(src, dst, slot, h).wait()
    energy_q = energy_of(q_own)
    energy_k = energy_of(k_own)
    line = lax.broadcasted_iota(jnp.int32, (8, rows), 0)
    message = jnp.where(line == 0, energy_q, 0.0)
    message = jnp.where(line == 1, energy_k, message)
    message = jnp.where(line == 2, reach_ref[0].astype(F32) * 0.25, message)
    message = jnp.where(line == 3, step_ref[0].astype(F32) * 0.25, message)
    est[tp] = message
    pl.semaphore_wait(barrier, len(greet) + len(opposite) * edge.astype(jnp.int32))

    def remote(src, dst, send, recv, to):
        return pltpu.make_async_remote_copy(
            src_ref=src, dst_ref=dst, send_sem=send, recv_sem=recv, device_id=to, device_id_type=MESH
        )

    up, down = shifted(1), shifted(-1)
    est_copies = [
        remote(est.at[tp], est.at[tp], est_s.at[i], est_r.at[tp], to) for i, to in enumerate(peers)
    ]

    def est_in(i):
        who = lax.rem(tp + i + 1, 4)
        return remote(est.at[who], est.at[who], est_s.at[i], est_r.at[who], peers[i])

    def q_copy(h):
        return remote(q_own.at[h], qa.at[h], q_s.at[h], q_r.at[h], up)

    def q_forward(h):
        return remote(qa.at[h], qb.at[h], qf_s.at[h], qf_r.at[h], up)

    def k_copy(h):
        return remote(k_own.at[h], k1.at[h], k_s.at[h], k_r.at[h], down)

    def v_copy(h):
        return remote(
            vt_own.at[h, pl.ds(0, HD), :], vt1.at[h, pl.ds(0, HD), :], v_s.at[h], v_r.at[h], down
        )

    def k_forward(h):
        return remote(k1.at[h], k2.at[h], kf_s.at[h], kf_r.at[h], down)

    def v_forward(h):
        return remote(
            vt1.at[h, pl.ds(0, HD), :], vt2.at[h, pl.ds(0, HD), :], vf_s.at[h], vf_r.at[h], down
        )

    def os_copy(h):
        return remote(os_out.at[h], os_in.at[h], os_s.at[h], os_r.at[h], up)

    def os_stat_copy(h):
        return remote(os_stat.at[h], os_in_stat.at[h], oss_s.at[h], oss_r.at[h], up)

    def far_copy(h):
        return remote(far_out.at[h], far_in.at[h], far_s.at[h], far_r.at[h], down)

    def far_stat_copy(h):
        return remote(far_stat.at[h], far_in_stat.at[h], fars_s.at[h], fars_r.at[h], down)

    parts = res_s.shape[0]
    part_rows = rows // parts

    def res_copy(i):
        cut = pl.ds(i * part_rows, part_rows)
        return remote(res_hbm.at[cut], res.at[cut], res_s.at[i], res_r.at[i], up)

    def st_copy(i, by):
        return remote(st_own, st_in.at[i], st_s.at[i], st_r.at[i], shifted(by))

    sibling = (tm, lo * 2 + 1 - core)

    def w_sibling():
        return remote(
            w_hbm.at[:, :, pl.ds(pl.multiple_of(sibling[1] * out_cols, HD), out_cols)],
            wbuf.at[:, tp],
            wsib_s,
            wsib_r,
            sibling,
        )

    def piece_rows(piece):
        return pl.ds(pl.multiple_of(piece * strip, strip), strip)

    def w_rows(side):
        return pl.ds(pl.multiple_of(y * strip + side * half, half), half)

    def w_import(side, c, part, some):
        to = sides[side][c]
        these = pl.ds(0, some)
        return remote(
            w_hbm.at[
                these, w_rows(part), pl.ds(pl.multiple_of(to[1] * out_cols, HD), out_cols)
            ],
            wbuf.at[these, tp, w_rows(part), :],
            wx_s.at[side, c],
            wx_r.at[side, core],
            to,
        )

    def w_import_in(side, c, part, some):
        slot = wbuf.at[pl.ds(0, some), (1 - lo) * 2 + c, w_rows(part), :]
        return remote(slot, slot, wx_s.at[side, c], wx_r.at[side, c], sides[side][c])

    def w_exports(act):
        @pl.when(inner)
        def _():
            for side in (0, 1):
                for c in (0, 1):
                    act(w_import(side, c, side, heads))

        for side in (0, 1):

            @pl.when(jnp.logical_and(edge, core == side))
            def _():
                for c in (0, 1):
                    act(w_import(side, c, 0, sideways))

    def w_piece(piece, h):
        return wbuf.at[h, pl.ds((1 - lo) * 2, 2), piece_rows(piece), :]

    def w_outward(h, to, rows_there):
        slot = wbuf.at[h, pl.ds((1 - lo) * 2, 2), rows_there, :]
        return remote(slot, slot, wz_s.at[h], wz_r.at[h], to)

    def outward(h, to, act):
        @pl.when(h < sideways)
        def _():
            act(w_outward(h, to, w_rows(1)))

        @pl.when(h >= sideways)
        def _():
            act(w_outward(h, to, piece_rows(y)))

    def w_along(k, h):
        slot = w_piece(lax.rem(y - turn_y * k + 4, 4), h)
        return remote(slot, slot, wy_s.at[k, h], wy_r.at[k, h], y_next)

    def w_along_in(k, h):
        slot = w_piece(lax.rem(y - turn_y * (k + 1) + 8, 4), h)
        return remote(slot, slot, wy_s.at[k, h], wy_r.at[k, h], y_next)

    half_rows = rows // 2

    def ag_slot(h, who, cut):
        return ag.at[h, who, cut]

    def unit(u):
        if isinstance(u, int) and u >= heads - 1:
            return heads - 1, pl.ds((u - heads + 1) * half_rows, half_rows)
        return u, pl.ds(0, rows)

    partner = (tm, (1 - lo) * 2 + core)
    diagonal = (1 - lo) * 2 + 1 - core

    def ag_move(i, u, who, to):
        h, cut = unit(u)
        slot = ag_slot(h, who, cut)
        return remote(slot, slot, ag_s.at[i, u], ag_r.at[who, u], to)

    def ag_copies(u):
        return [
            ag_move(0, u, tp, partner),
            ag_move(1, u, tp, sibling),
            ag_move(2, u, partner[1], sibling),
        ]

    def each(body):
        @pl.loop(0, heads)
        def _(h):
            body(h)

    def begin_up(some, end):
        @pl.loop(some, end)
        def _(h):
            q_copy(h).start()

    def begin_keys():
        for h in range(early):
            k_copy(h).start()

    def begin_values():
        for h in range(early):
            v_copy(h).start()

    def begin_rest():
        @pl.loop(early, heads)
        def _(h):
            k_copy(h).start()
            v_copy(h).start()

    early = 2
    for copy in est_copies:
        copy.start()
    pl.when(jnp.logical_not(first))(begin_keys)

    @pl.when(jnp.logical_not(last))
    def _():
        begin_up(0, early)

    w_exports(lambda copy: copy.start())

    for i in range(3):
        est_in(i).wait_recv()

    @pl.when(edge)
    def _():
        for side in (0, 1):
            w_import_in(side, side, 0, sideways).wait_recv()
        for other in opposite:
            pl.semaphore_signal(gate_sem, inc=1, device_id=other, device_id_type=MESH)

    st_own[...] = est[0] + est[1] + est[2] + est[3]
    st_moves = [(0, 1), (1, 2), (2, -1), (3, -2)]
    for i, by in st_moves:
        st_copy(i, by).start()

    ones = jnp.ones((16, rows), BF16)
    for h in range(heads):
        load(v_hbm, v_own, 2, h).wait()
        vt_own[h, :HD, :] = jnp.transpose(v_own[h])
        vt_own[h, HD : HD + 16, :] = ones
        if h == early - 1:
            pl.when(jnp.logical_not(first))(begin_values)

    @pl.when(jnp.logical_not(last))
    def _():
        begin_up(early, heads)

    pl.when(jnp.logical_not(first))(begin_rest)
    for h in range(heads):
        both = q_gain_ref[h * HD : (h + 1) * HD] * k_gain_ref[h * HD : (h + 1) * HD]
        gain_buf[h] = both * (HD ** (-0.5) * LOG2E)
        vt1[h, HD : HD + 16, :] = ones
        vt2[h, HD : HD + 16, :] = ones

    def pass_weights():
        for side in (0, 1):
            for c in (0, 1):
                w_import_in(side, c, side, heads).wait_recv()

        @pl.loop(0, heads)
        def _(h):
            w_along(0, h).start()

            @pl.when(z == 1)
            def _():
                outward(h, down, lambda copy: copy.start())

            @pl.when(z == 6)
            def _():
                outward(h, up, lambda copy: copy.start())

    pl.when(inner)(pass_weights)

    @pl.when(edge)
    def _():
        pl.semaphore_wait(gate_sem, len(opposite))

    @pl.when(last)
    def _():
        begin_up(0, heads)

    @pl.when(first)
    def _():
        begin_keys()
        begin_values()
        begin_rest()

    w_sibling().start()
    def begin_residual():
        for i in range(parts // 2):
            res_copy(i).start()

    pl.when(z != 6)(begin_residual)

    def column(state, row):
        scale = lax.rsqrt(state[row : row + 1, :] / width + EPS)
        return jnp.transpose(jnp.broadcast_to(scale, (HD, rows)))

    def unit_q(raw, scale, h):
        return (raw.astype(F32) * scale * gain_buf[pl.ds(h, 1), :]).astype(BF16)

    def unit_k(raw, scale):
        return (raw.astype(F32) * scale).astype(BF16)

    def scores_of(keys, queries):
        return lax.dot_general(
            keys, queries, (((1,), (1,)), ((), ())), preferred_element_type=F32
        )

    def alone(keys, queries, values):
        scores = scores_of(keys, queries)
        peak = jnp.max(scores, axis=0, keepdims=True)
        weight = jnp.exp2(scores - peak).astype(BF16)
        return jnp.dot(values, weight, preferred_element_type=F32), peak

    fold = rows // HD

    def pair(first, second):
        return jnp.concatenate(
            [one[:, i * HD : (i + 1) * HD] for one in (first, second) for i in range(fold)], axis=0
        )

    def unpair(packed):
        first = jnp.concatenate([packed[i : i + 1] for i in range(fold)], axis=1)
        second = jnp.concatenate([packed[fold + i : fold + i + 1] for i in range(fold)], axis=1)
        return first, second

    q_scale = column(st_own, 0)
    k_scale = column(st_own, 1)

    def self_part(h):
        q_copy(h).wait_recv()
        q_forward(h).start()
        kn[h] = unit_k(k_own[h], k_scale)
        mixed, peak = alone(kn[h], unit_q(q_own[h], q_scale, h), vt_own[h])
        os_out[h] = mixed[:HD].astype(BF16)
        os_stat[h] = pair(peak, mixed[HD : HD + 1])
        os_copy(h).start()
        os_stat_copy(h).start()

    each(self_part)
    pl.when(z == 6)(begin_residual)
    for i in range(parts // 2, parts):
        res_copy(i).start()

    st_copy(0, 1).wait_recv()
    state_a = st_in.at[0]
    reach = state_a[2:3, :]
    step = state_a[3:4, :1]
    place = lax.rem(pos_ref[0] + spans - 1, spans)

    def live(distance):
        inside = (place + distance <= spans - 1).astype(F32)
        return jnp.logical_and(reach >= distance, inside > 0.5)

    qa_scale = column(state_a, 0)

    def near_part(h):
        qn[h] = unit_q(qa[h], qa_scale, h)
        scores = scores_of(kn[h], qn[h])
        allowed = live(1)
        peak = jnp.max(scores, axis=0, keepdims=True)
        weight = jnp.exp2(scores - jnp.where(allowed, peak, MANY)).astype(BF16)
        acc[h] = jnp.dot(vt_own[h], weight, preferred_element_type=F32)
        top[h] = jnp.broadcast_to(jnp.where(allowed, peak, FEW), (8, rows))

    each(near_part)

    def join(h, keys, values, allowed):
        scores = scores_of(keys, qn[h])
        before = top[h][:1]
        peak = jnp.where(allowed, jnp.max(scores, axis=0, keepdims=True), FEW)
        after = jnp.maximum(before, peak)
        weight = jnp.exp2(scores - jnp.where(allowed, after, MANY)).astype(BF16)
        acc[h] = acc[h] * jnp.exp2(before - after) + jnp.dot(
            values, weight, preferred_element_type=F32
        )
        top[h] = jnp.broadcast_to(after, (8, rows))

    st_copy(2, -1).wait_recv()
    k1_scale = column(st_in.at[2], 1)

    def second_part(h):
        k_copy(h).wait_recv()
        k_forward(h).start()
        v_copy(h).wait_recv()
        v_forward(h).start()
        join(h, unit_k(k1[h], k1_scale), vt1[h], live(2))

        @pl.when(edge)
        def _():
            outward(h, up, lambda copy: copy.wait_recv())
            w_along(0, h).start()

    each(second_part)

    st_copy(1, 2).wait_recv()
    st_copy(3, -2).wait_recv()
    qb_scale = column(st_in.at[1], 0)
    k2_scale = column(st_in.at[3], 1)

    def third_part(h):
        q_forward(h).wait_recv()
        k_forward(h).wait_recv()
        v_forward(h).wait_recv()
        keys = unit_k(k2[h], k2_scale)
        mixed, peak = alone(keys, unit_q(qb[h], qb_scale, h), vt2[h])
        far_out[h] = mixed[:HD].astype(BF16)
        far_stat[h] = pair(peak, mixed[HD : HD + 1])
        far_copy(h).start()
        far_stat_copy(h).start()
        join(h, keys, vt2[h], live(3))
        w_along_in(0, h).wait_recv()
        w_along(1, h).start()

        @pl.when(h > 0)
        def _():
            w_along_in(1, h - 1).wait_recv()
            w_along(2, h - 1).start()

    each(third_part)
    w_along_in(1, heads - 1).wait_recv()
    w_along(2, heads - 1).start()

    def tiles(body):
        @pl.loop(0, out_cols // 256)
        def _(j):
            body(pl.ds(pl.multiple_of(j * 256, 256), 256))

    def product(h, cut):
        left = jnp.concatenate([ag[h, i] for i in range(4)], axis=1)
        return jnp.dot(left, wbuf[h, :, :, cut].reshape(4 * HD, 256), preferred_element_type=F32)

    def project(h):
        ag_move(0, h, sibling[1], sibling).wait_recv()
        ag_move(0, h, diagonal, sibling).wait_recv()
        w_along_in(2, h).wait_recv()

        def body(cut):
            total[:, cut] = total[:, cut] + product(h, cut)

        tiles(body)

    total[...] = jnp.zeros_like(total)

    def arrived(h):
        os_copy(h).wait_recv()
        os_stat_copy(h).wait_recv()
        far_copy(h).wait_recv()
        far_stat_copy(h).wait_recv()

    def merge(u):
        h, _ = unit(u)
        cut = slice(0, rows)
        if isinstance(u, int) and u >= heads - 1:
            cut = slice((u - heads + 1) * half_rows, (u - heads + 2) * half_rows)
        peak_s, sum_s = (one[:, cut] for one in unpair(os_in_stat[h]))
        peak_f, sum_f = (one[:, cut] for one in unpair(far_in_stat[h]))
        peak_m = top[h, :1, cut]
        peak_f = jnp.where(live(4)[:, cut], peak_f, FEW)
        peak = jnp.maximum(jnp.maximum(peak_s, peak_m), peak_f)
        by_s, by_m, by_f = jnp.exp2(peak_s - peak), jnp.exp2(peak_m - peak), jnp.exp2(peak_f - peak)
        mixed = acc[h, :, cut]
        whole = sum_s * by_s + mixed[HD : HD + 1] * by_m + sum_f * by_f
        share = 1.0 / whole
        attended = (
            os_in[h, :, cut].astype(F32) * (by_s * share)
            + mixed[:HD] * (by_m * share)
            + far_in[h, :, cut].astype(F32) * (by_f * share)
        )
        ag[h, tp, cut] = jnp.transpose(attended).astype(BF16)
        for copy in ag_copies(u)[:2]:
            copy.start()

    def relay(u):
        ag_move(0, u, partner[1], partner).wait_recv()
        ag_copies(u)[2].start()

    w_own_copy.wait()
    w_sibling().wait_recv()
    final = heads - 1
    for h in range(final):
        arrived(h)
        merge(h)
        if h >= 2:
            relay(h - 2)
        if h >= 3:
            project(h - 3)
    arrived(final)
    merge(final)
    merge(final + 1)
    for h in range(final - 2, final):
        relay(h)
        project(h - 1)
    for i in range(parts):
        res_copy(i).wait_recv()
    fresh_copy.wait()
    table = gate_ref[...].astype(F32)
    pick = lax.broadcasted_iota(jnp.int32, table.shape, 0).astype(F32) == step
    gate_buf[...] = jnp.sum(jnp.where(pick, table, 0.0), axis=0, keepdims=True)
    relay(final)
    relay(final + 1)
    project(final - 1)
    w_along_in(2, final).wait_recv()

    for u in (final, final + 1):
        ag_move(0, u, sibling[1], sibling).wait_recv()
        ag_move(0, u, diagonal, sibling).wait_recv()
        part = slice((u - final) * half_rows, (u - final + 1) * half_rows)

        def finish(cut, part=part):
            right = wbuf[final, :, :, cut].reshape(4 * HD, 256)
            left = jnp.concatenate([ag[final, i, part] for i in range(4)], axis=1)
            last_term = jnp.dot(left, right, preferred_element_type=F32)
            projected = total[part, cut] + last_term
            updated = (res[part, cut].astype(F32) + gate_buf[:, cut] * projected).astype(BF16)
            newest = jnp.full(updated.shape, pos_ref[0], jnp.int32) == 0
            out_ref[part, cut] = jnp.where(newest, fresh[part, cut], updated)

        tiles(finish)

    for copy in est_copies:
        copy.wait_send()
    for i, by in st_moves:
        st_copy(i, by).wait_send()
    for i in range(parts):
        res_copy(i).wait_send()
    w_sibling().wait_send()

    w_exports(lambda copy: copy.wait_send())

    @pl.when(jnp.logical_or(z == 1, z == 6))
    def _():
        @pl.loop(0, heads)
        def _(h):
            outward(h, down, lambda copy: copy.wait_send())

    def sent(h):
        for copy in (
            q_copy,
            q_forward,
            k_copy,
            v_copy,
            k_forward,
            v_forward,
            os_copy,
            os_stat_copy,
            far_copy,
            far_stat_copy,
        ):
            copy(h).wait_send()
        for i in range(3):
            w_along(i, h).wait_send()

    each(sent)
    for u in range(heads + 1):
        for copy in ag_copies(u):
            copy.wait_send()


def local(
    queries,
    key_rows,
    value_rows,
    query_gain,
    key_gain,
    out_weight,
    residual,
    gate_table,
    timesteps,
    windows,
    queue_positions,
    fresh_span,
):
    spans = lax.axis_size("tm")
    rows, width = queries.shape
    heads = width // HD
    out_cols = residual.shape[1]
    weight = out_weight.reshape(heads, HD, out_weight.shape[1])
    chunk = pltpu.VMEM((heads, rows, HD), BF16)
    flat = pltpu.VMEM((heads, HD, rows), BF16)
    tall = pltpu.VMEM((heads, HD + 16, rows), BF16)
    stats = pltpu.VMEM((heads, 8, rows), F32)
    packed = pltpu.VMEM((heads, 2 * (rows // HD), HD), F32)
    one = pltpu.SemaphoreType.DMA
    per_head = one((heads,))
    parts = 4
    hbm = pl.BlockSpec(memory_space=pl.ANY)
    vmem = pl.BlockSpec(memory_space=pltpu.VMEM)
    smem = pl.BlockSpec(memory_space=pltpu.SMEM)

    def run(*operands):
        def body(*refs):
            kernel(spans, *refs)

        return pl.pallas_call(
            body,
            out_shape=pltpu.VMEM((rows, out_cols), BF16),
            in_specs=[hbm, hbm, hbm, vmem, vmem, hbm, hbm, vmem, hbm, smem, smem, smem],
            out_specs=vmem,
            scratch_shapes=[
                chunk,
                chunk,
                chunk,
                tall,
                chunk,
                chunk,
                chunk,
                chunk,
                chunk,
                tall,
                chunk,
                tall,
                pltpu.VMEM((4, 8, rows), F32),
                pltpu.VMEM((8, rows), F32),
                pltpu.VMEM((4, 8, rows), F32),
                flat,
                packed,
                flat,
                packed,
                flat,
                packed,
                flat,
                packed,
                pltpu.VMEM((heads, HD + 16, rows), F32),
                stats,
                pltpu.VMEM((heads, 4, rows, HD), BF16),
                pltpu.VMEM((heads, 4, HD, out_cols), BF16),
                pltpu.VMEM((rows, out_cols), BF16),
                pltpu.VMEM((rows, out_cols), F32),
                pltpu.VMEM((heads, HD), F32),
                pltpu.VMEM((1, out_cols), F32),
                pltpu.VMEM((rows, out_cols), BF16),
                one((3, heads)),
                one,
                one,
                one((3,)),
                one((4,)),
                one((4,)),
                one((4,)),
                per_head,
                per_head,
                per_head,
                per_head,
                per_head,
                per_head,
                per_head,
                per_head,
                per_head,
                per_head,
                per_head,
                per_head,
                per_head,
                per_head,
                per_head,
                per_head,
                per_head,
                per_head,
                per_head,
                per_head,
                one((parts,)),
                one((parts,)),
                one,
                one,
                one((2, 2)),
                one((2, 2)),
                one((3, heads)),
                one((3, heads)),
                one((3, heads + 1)),
                one((4, heads + 1)),
                per_head,
                per_head,
                pltpu.SemaphoreType.REGULAR,
            ],
            compiler_params=pltpu.CompilerParams(
                collective_id=0, has_side_effects=True, vmem_limit_bytes=56 * 2**20
            ),
            name="window_block",
        )(*operands)

    return run(
        queries,
        key_rows,
        value_rows,
        query_gain,
        key_gain,
        weight,
        residual,
        gate_table,
        fresh_span,
        timesteps,
        windows,
        queue_positions,
    )


def solution(mesh):
    placed = (
        P("tm", "tp"),
        P("tm", "tp"),
        P("tm", "tp"),
        P("tp"),
        P("tp"),
        P("tp", None),
        P("tm", "tp"),
        P(None, "tp"),
        P("tm"),
        P("tm"),
        P("tm"),
        P(None, "tp"),
    )
    return jax.shard_map(
        local, mesh=mesh, in_specs=placed, out_specs=P("tm", "tp"), check_vma=False
    )
```
